32 devices in a mesh: wide: 8 (over z, y), narrow: 4 (over x, core).
Axes of the slice: x: 2, y: 2, z: 4, core: 2. Of those that a mesh axis runs over, the one named last changes fastest.
Arguments:
- atm_state: float32 [144, 65536], P(None, ('wide', 'narrow')), may hold values from -6 to 6
- group_owner: int32 [65536, 1], P(('wide', 'narrow')), may hold values from 0 to 31; in each aligned block of 2048 rows (0 to 2047, 2048 to 4095, ...) at most 128 rows name the same one
- regime_ops: bfloat16 [32, 4, 144, 144], P(('wide', 'narrow')), may hold values from -0.5 to 0.5
- flux_map: bfloat16 [144, 4], replicated, may hold values from -0.5 to 0.5
- remap_src: int32 [4, 256, 1024], P(None, 'wide', 'narrow'), may hold values from 0 to 8
- remap_weight: float32 [4, 256, 1024], P(None, 'wide', 'narrow'), may hold values from 0.05 to 0.6
- ocean_mask: int32 [256, 1024], P('wide', 'narrow'), may hold values 0 or 1
- tracer: float32 [62, 256, 1024], P(None, 'wide', 'narrow'), may hold values from -6 to 6
- surface_height: float32 [256, 1024], P('wide', 'narrow'), may hold values from -3 to 3
- transports: float32 [2, 256, 1024], P(None, 'wide', 'narrow'), may hold values from -3 to 3
Outputs:
- atm_new: float32 [144, 65536], P(None, ('wide', 'narrow'))
- tracer_new: float32 [62, 256, 1024], P(None, 'wide', 'narrow')
- height_new: float32 [256, 1024], P('wide', 'narrow')
- transports_new: float32 [2, 256, 1024], P(None, 'wide', 'narrow')
The draws below stay inside these ranges and needn't reach their ends.
Inputs may be any that keep to these rules, and one draw needn't show every extreme that they name: `group_owner`: among the 2048 columns of one device no owner is named more than 128 times, and one is named exactly 128 times.
All inputs are finite; a program needn't handle non-finite values. No bound on the sum of `ocean_mask` on one device may be relied on, other than what follows from the above.
Results may differ from the reference program's by a relative error of at most 0.0043.
Values may be sent and summed in bfloat16 or wider, within the bound.
A program may use at most 128 MiB of HBM per device.

```python
import math
import jax
import jax.numpy as jnp
import numpy as np
from jax import lax

LO = 62
AR = 16
AC = 128
NPHYS = 4
NSUB = 4
REMAP_K = 4
NFLUX = 4
F = 144
COLS_DEV = 2048
CAP = 128
COLUMNS = 65536
NAR = 128
NAC = 512
NOR = 256
NOC = 1024
N_NARROW = 4
DEVICES = 32


def with_ends(entries, rng, low, high):
    dims = entries.shape
    index_at = [jax.random.randint(jax.random.fold_in(rng, axis), (), 0, dims[axis]) for axis in range(len(dims))]
    entries = entries.at[tuple(index_at)].set(low)
    longest = dims.index(max(dims))
    index_at[longest] = (index_at[longest] + 1) % dims[longest]
    return entries.at[tuple(index_at)].set(high)


def steps_of(stream_key, dims, cuts, low, high):
    factor_of = 1.0
    for position, shards_of in cuts:
        draws = jax.random.uniform(jax.random.fold_in(jax.random.fold_in(stream_key, 6), position), (shards_of,), jnp.float32, low / len(cuts), high / len(cuts))
        factor_of = factor_of * jnp.repeat(jnp.exp(draws), dims[position] // shards_of).reshape((-1,) + (1,) * (len(dims) - 1 - position))
    return factor_of


def shared_out(stream_key, own, number, rows, number_of, top, bound, lean):
    order = jax.random.permutation(stream_key, number_of)
    crowded, ordinary = shares(number_of, rows * top, bound, lean, True), shares(number_of, rows * top, bound, lean, False)
    places = jnp.arange(number_of)

    def named(sizes, turn):
        used = int((sizes > 0).sum())
        fixed = max(1, used // 4)
        moved = fixed + (places - fixed + turn * (used - fixed)) % max(1, number_of - fixed)
        return jnp.zeros((number_of,), jnp.int32).at[order[jnp.where(places < fixed, places, moved)]].set(jnp.asarray(sizes, jnp.int32))

    sizes = jnp.where(number % 4 == 0, named(crowded, number // 4), named(ordinary, number - number // 4 - 1))
    mixed = jax.random.permutation(jax.random.fold_in(own, 3), number_of)
    donor, receiver = mixed[0:number_of // 2 * 2:2], mixed[1:number_of // 2 * 2:2]
    margin = jnp.minimum(sizes[donor] - 1, bound - sizes[receiver]) // 2
    margin = jnp.where((donor == order[0]) | (receiver == order[0]) | (sizes[receiver] == 0), 0, jnp.maximum(margin, 0))
    moved = jax.random.randint(jax.random.fold_in(own, 4), (number_of // 2,), 0, 1 << 20) % (margin + 1)
    sizes = sizes.at[donor].add(-moved).at[receiver].add(moved)
    items = jnp.searchsorted(jnp.cumsum(sizes), jnp.arange(rows * top), side="right").astype(jnp.int32)
    listing = items.reshape(top, rows).T
    listing = listing[jax.random.permutation(jax.random.fold_in(own, 1), rows)]
    turn = jax.random.randint(jax.random.fold_in(own, 2), (rows, 1), 0, top)
    return jnp.take_along_axis(listing, (jnp.arange(top)[None, :] + turn) % top, axis=1)


def shares(number_of, total, most, skew, full):
    weights = [(1 << 20) // math.isqrt(grade ** skew) + 1 for grade in range(1, number_of + 1)]
    largest = most if full else min(most, max(-(-total // number_of), total * weights[0] // sum(weights)))
    least = 1 if total - largest >= number_of - 1 else 0
    holding, surplus = [largest] + [least] * (number_of - 1), total - largest - least * (number_of - 1)
    while surplus > 0:
        movable = [i for i in range(1, number_of) if holding[i] < largest] or [i for i in range(1, number_of) if holding[i] < most]
        mass, budget = sum([weights[i] for i in movable]), surplus
        for i in movable:
            addition = min(most - holding[i], max(1, budget * weights[i] // mass), surplus)
            holding[i] = holding[i] + addition
            surplus = surplus - addition
    return np.array(holding)


def scatter_about(stream_key, extent, deviation, limit, pieces=(), kind=jnp.bfloat16):
    drawn = jax.random.normal(stream_key, extent, jnp.float32) * deviation
    if len(pieces) > 0:
        drawn = steps_of(stream_key, extent, pieces, -0.22, 0.18) * drawn
    return jnp.clip(drawn, min=-limit, max=limit).astype(kind)


def setup_inputs(seed: int = 0) -> dict:
    key_list = jax.random.split(jax.random.key(seed), 11)
    atm_state = scatter_about(key_list[0], (F, COLUMNS), 1.0, 6.0, ((1, 32),), jnp.float32)
    group_owner_keys = jax.random.split(jax.random.fold_in(key_list[1], 1), COLUMNS // COLS_DEV)
    group_owner_turns = jax.random.permutation(jax.random.fold_in(key_list[1], 3), COLUMNS // COLS_DEV)
    group_owner = jax.vmap(lambda own, number: shared_out(jax.random.fold_in(key_list[1], 2), own, number, COLS_DEV, DEVICES, 1, CAP, 2))(group_owner_keys, group_owner_turns).reshape((COLUMNS, 1))
    regime_ops = scatter_about(key_list[2], (DEVICES, NPHYS, F, F), F ** -0.5, 0.5, ((0, 32),))
    flux_map = scatter_about(key_list[3], (F, NFLUX), F ** -0.5, 0.5)
    remap_src = with_ends(jax.random.randint(key_list[4], (REMAP_K, NOR, NOC), 0, 9), jax.random.fold_in(key_list[4], 1), 0, 8).astype(jnp.int32)
    remap_weight = jnp.clip(jnp.exp(math.log(0.6) - 2.4849067 * jax.random.uniform(key_list[5], (REMAP_K, NOR, NOC), jnp.float32) ** steps_of(key_list[5], (REMAP_K, NOR, NOC), ((1, 8), (2, 4)), -0.2, 0.2)), 0.05, 0.6)
    ocean_mask = with_ends((jax.random.randint(key_list[6], (NOR, NOC), 0, 4) < 3).astype(jnp.int32), jax.random.fold_in(key_list[6], 1), 0, 1)
    tracer = scatter_about(key_list[7], (LO, NOR, NOC), 1.0, 6.0, ((1, 8), (2, 4)), jnp.float32)
    surface_height = scatter_about(key_list[8], (NOR, NOC), 0.5, 3.0, ((0, 8), (1, 4)), jnp.float32)
    transports = scatter_about(key_list[9], (2, NOR, NOC), 0.5, 3.0, ((1, 8), (2, 4)), jnp.float32)
    return dict(atm_state=atm_state, group_owner=group_owner, regime_ops=regime_ops, flux_map=flux_map, remap_src=remap_src, remap_weight=remap_weight, ocean_mask=ocean_mask, tracer=tracer, surface_height=surface_height, transports=transports)


relax_rate = 0.5
kappa_mix = 0.2
heat_gain = 0.5
gravity = 0.7
depth_mean = 0.7
wind_gain = 0.3
fresh_gain = 0.3


def column_ranks(owners, peers):
    onehot = (owners[:, None] == jnp.arange(peers, dtype=jnp.int32)[None, :]).astype(jnp.int32)
    before = jnp.cumsum(onehot, axis=0) - onehot
    return jnp.sum(before * onehot, axis=1)


def physics(operators, columns, flux_map):
    initial = columns.astype(jnp.float32)
    current = initial
    for sweep in range(operators.shape[0]):
        mixed = lax.dot_general(operators[sweep], current.astype(jnp.bfloat16), (((0,), (0,)), ((), ())), preferred_element_type=jnp.float32)
        current = current + relax_rate * jnp.tanh(mixed)
    final = current.astype(jnp.bfloat16)
    tendency = (current - initial).astype(jnp.bfloat16)
    fluxes = lax.dot_general(flux_map, final, (((0,), (0,)), ((), ())), preferred_element_type=jnp.float32).astype(jnp.bfloat16)
    return tendency, fluxes


def diffuse(tracer_ext, mask_ext):
    centre = tracer_ext[:, 1:-1, 1:-1]
    mask_centre = mask_ext[:, 1:-1, 1:-1]
    summed = jnp.zeros_like(centre)
    cuts = ((slice(2, None), slice(1, -1)), (slice(None, -2), slice(1, -1)), (slice(1, -1), slice(2, None)), (slice(1, -1), slice(None, -2)))
    for row_cut, col_cut in cuts:
        summed = summed + mask_centre * mask_ext[:, row_cut, col_cut] * (tracer_ext[:, row_cut, col_cut] - centre)
    return centre + kappa_mix * summed


def momentum(flow, height, height_next, mask, mask_next, stress):
    return mask * mask_next * (flow - gravity * (height_next - height) + wind_gain * stress)


def continuity(height, flow_u, flow_u_west, flow_v, flow_v_south, mask, fresh):
    return mask * (height - depth_mean * ((flow_u - flow_u_west) + (flow_v - flow_v_south)) + fresh_gain * fresh)


def subcycles(height, flow_u, flow_v, mask, forcing, count):
    padded_mask = jnp.pad(mask, 1)
    mask_east = padded_mask[1:-1, 2:]
    mask_north = padded_mask[2:, 1:-1]
    for substep in range(count):
        padded_height = jnp.pad(height, 1)
        flow_u = momentum(flow_u, height, padded_height[1:-1, 2:], mask, mask_east, forcing[1])
        flow_v = momentum(flow_v, height, padded_height[2:, 1:-1], mask, mask_north, forcing[2])
        padded_u = jnp.pad(flow_u, 1)
        padded_v = jnp.pad(flow_v, 1)
        height = continuity(height, flow_u, padded_u[1:-1, :-2], flow_v, padded_v[:-2, 1:-1], mask, forcing[0])
    return height, flow_u, flow_v


def reference(atm_state, group_owner, regime_ops, flux_map, remap_src, remap_weight, ocean_mask, tracer, surface_height, transports):
    owners = group_owner[:, 0]

    def block_ranks(block_owners):
        return column_ranks(block_owners, DEVICES)

    ranks = jax.vmap(block_ranks)(owners.reshape(DEVICES, COLS_DEV)).reshape(-1)
    sources = jnp.arange(COLUMNS, dtype=jnp.int32) // COLS_DEV
    slots = owners * (DEVICES * CAP) + sources * CAP + ranks
    initial = atm_state.astype(jnp.bfloat16)
    buffer = jnp.zeros((F, DEVICES * DEVICES * CAP), jnp.bfloat16).at[:, slots].set(initial)
    per_owner = buffer.reshape(F, DEVICES, DEVICES * CAP).transpose(1, 0, 2)

    def run_owner(pair):
        return physics(pair[0], pair[1], flux_map)

    tendency, fluxes = lax.map(run_owner, (regime_ops, per_owner))
    tend_cols = tendency.transpose(1, 0, 2).reshape(F, -1)[:, slots]
    flux_cols = fluxes.transpose(1, 0, 2).reshape(NFLUX, -1)[:, slots].astype(jnp.float32)
    atm_new = atm_state + tend_cols.astype(jnp.float32)
    rows_here = jnp.arange(NOR, dtype=jnp.int32)[None, :, None] // 2
    cols_here = jnp.arange(NOC, dtype=jnp.int32)[None, None, :] // 2
    atm_row = jnp.clip(rows_here + remap_src // 3 - 1, 0, NAR - 1).astype(jnp.int32)
    atm_col = jnp.clip(cols_here + remap_src % 3 - 1, 0, NAC - 1).astype(jnp.int32)
    source_col = ((atm_row // AR) * N_NARROW + atm_col // AC) * COLS_DEV + (atm_row % AR) * AC + atm_col % AC
    ocean_flux = jnp.sum(flux_cols[:, source_col.astype(jnp.int32)] * remap_weight[None], axis=1)
    mask = ocean_mask.astype(jnp.float32)
    tracer_ext = jnp.pad(tracer, ((0, 0), (1, 1), (1, 1)))
    mask_ext = jnp.pad(mask[None], ((0, 0), (1, 1), (1, 1)))
    tracer_new = diffuse(tracer_ext, mask_ext)
    tracer_new = tracer_new.at[0].add(heat_gain * mask * ocean_flux[0])
    height, flow_u, flow_v = subcycles(surface_height, transports[0], transports[1], mask, ocean_flux[1:], NSUB)
    return atm_new, tracer_new, height, jnp.stack([flow_u, flow_v])
```

```python
import functools

import jax
import jax.numpy as jnp
from jax import lax
from jax.experimental import pallas as pl
from jax.experimental.pallas import tpu as pltpu
from jax.sharding import PartitionSpec as P

AC = 128
NSUB = 4
LANES = 128
CHUNK = 512
VMEM_BYTES = 48 * 1024 * 1024

relax_rate = 0.5
kappa_mix = 0.2
heat_gain = 0.5
gravity = 0.7
depth_mean = 0.7
wind_gain = 0.3
fresh_gain = 0.3

f32 = jnp.float32
bf16 = jnp.bfloat16
i32 = jnp.int32
MESH = pl.DeviceIdType.MESH
SIDES = ((1, 0), (-1, 0), (0, 1), (0, -1), (1, 1), (1, -1), (-1, 1), (-1, -1))
VMEM = pl.BlockSpec(memory_space=pltpu.VMEM)


def iota(shape, dim):
    return lax.broadcasted_iota(i32, shape, dim)


def place_kernel(peers, capacity, owner_ref, atm_ref, xs_ref, slot_ref):
    count = owner_ref.shape[1]
    upper = (iota((LANES, LANES), 0) < iota((LANES, LANES), 1)).astype(bf16)
    ids = iota((peers, LANES), 0)
    carry = jnp.zeros((peers, 1), f32)
    for start in range(0, count, LANES):
        owner = owner_ref[:, start : start + LANES]
        hot = (ids == owner).astype(f32)
        before = jnp.dot(hot.astype(bf16), upper, preferred_element_type=f32) + carry
        rank = jnp.sum(hot * before, axis=0, keepdims=True)
        slot_ref[:, start : start + LANES] = owner * capacity + rank.astype(i32)
        carry = carry + jnp.sum(hot, axis=1, keepdims=True)
    columns = atm_ref[...].astype(bf16)

    def step(i, _):
        begin = pl.multiple_of(i * CHUNK, CHUNK)
        selector = (iota((CHUNK, count), 0) + begin == slot_ref[...]).astype(f32).astype(bf16)
        placed = lax.dot_general(
            columns, selector, (((1,), (1,)), ((), ())), preferred_element_type=f32
        )
        xs_ref[:, pl.ds(begin, CHUNK)] = placed.astype(bf16)
        return 0

    lax.fori_loop(0, xs_ref.shape[1] // CHUNK, step, 0)


def physics_kernel(sweeps, capacity, packed_rows, ops_ref, xs_ref, fm_ref, y_ref):
    features = xs_ref.shape[0]
    tail = features - LANES
    groups = CHUNK // capacity
    initial = [xs_ref[:, g * capacity : (g + 1) * capacity].astype(f32) for g in range(groups)]
    current = list(initial)
    for sweep in range(sweeps):
        for g in range(groups):
            base = g * packed_rows
            rounded = current[g].astype(bf16)
            parts = [rounded[:LANES]]
            if sweep > 0:
                parts.append(jnp.zeros((sweep * tail, capacity), bf16))
            parts.append(rounded[LANES:])
            parts.append(jnp.zeros((LANES - (sweep + 1) * tail, capacity), bf16))
            operand = jnp.concatenate(parts, axis=0)
            head = ops_ref[base + sweep * features : base + (sweep + 1) * features, :]
            rest = ops_ref[base + sweeps * features : base + (sweeps + 1) * features, :]
            matrix = jnp.concatenate([head, rest], axis=1)
            mixed = jnp.dot(matrix, operand, preferred_element_type=f32)
            current[g] = current[g] + relax_rate * jnp.tanh(mixed)
    for g in range(groups):
        cols = slice(g * capacity, (g + 1) * capacity)
        y_ref[:features, cols] = (current[g] - initial[g]).astype(bf16)
        fluxes = jnp.dot(fm_ref[...], current[g].astype(bf16), preferred_element_type=f32)
        y_ref[features:, cols] = fluxes.astype(bf16)


def fetch_kernel(y_ref, slot_ref, atm_ref, new_ref, flux_ref):
    features = atm_ref.shape[0]
    slots = y_ref.shape[1]
    selector = (iota((slots, slot_ref.shape[1]), 0) == slot_ref[...]).astype(f32).astype(bf16)
    returned = jnp.dot(y_ref[...], selector, preferred_element_type=f32)
    new_ref[...] = atm_ref[...] + returned[:features]
    flux_ref[...] = returned[features:]


def side_device(side):
    wide, narrow = lax.axis_size("wide"), lax.axis_size("narrow")
    return (
        lax.rem(lax.axis_index("wide") + side[0] + wide, wide),
        lax.rem(lax.axis_index("narrow") + side[1] + narrow, narrow),
    )


def greet():
    barrier = pltpu.get_barrier_semaphore()
    for side in SIDES:
        pl.semaphore_signal(barrier, inc=1, device_id=side_device(side), device_id_type=MESH)
    pl.semaphore_wait(barrier, len(SIDES))


def leaving(step, size, halo):
    if step > 0:
        return pl.ds(size - halo, halo)
    return pl.ds(0, halo) if step < 0 else pl.ds(0, size)


def landing(step, size, halo):
    if step > 0:
        return pl.ds(0, halo)
    return pl.ds(halo + size, halo) if step < 0 else pl.ds(halo, size)


def edge_copies(src, dst, halo_rows, halo_cols, send_sem, recv_sem):
    rows, cols = src.shape[1], src.shape[2]
    return [
        pltpu.make_async_remote_copy(
            src_ref=src.at[:, leaving(dr, rows, halo_rows), leaving(dc, cols, halo_cols)],
            dst_ref=dst.at[:, landing(dr, rows, halo_rows), landing(dc, cols, halo_cols)],
            send_sem=send_sem.at[k],
            recv_sem=recv_sem.at[k],
            device_id=side_device((dr, dc)),
            device_id_type=MESH,
        )
        for k, (dr, dc) in enumerate(SIDES)
    ]


HR = 8
HC = 128


def turned(x, shift, axis):
    return pltpu.roll(x, shift % x.shape[axis], axis)


def static_kernel(
    src_ref, weight_ref, mask_ref, tracer_ref, height_ref, flow_ref,
    wsum_ref, planes_ref, tracer_out_ref,
    own, ext, row_out, row_in, col_out, col_in,
    send_sem, recv_sem, tsend_sem, trecv_sem,
):
    entries, rows, cols = src_ref.shape
    levels = tracer_ref.shape[0]
    own[0] = mask_ref[...].astype(f32)
    own[1] = height_ref[...]
    own[2] = flow_ref[0]
    own[3] = flow_ref[1]
    for e in range(entries):
        own[4 + e] = src_ref[e].astype(f32)
        own[4 + entries + e] = weight_ref[e]
    ext[:, HR : HR + rows, HC : HC + cols] = own[...]
    greet()
    copies = edge_copies(own, ext, HR, HC, send_sem, recv_sem)
    for copy in copies:
        copy.start()

    lane = iota((rows, LANES), 1)

    def pack(level, carry):
        first, last = carry
        field = tracer_ref[level]
        row_out[0, pl.ds(level, 1), :] = field[rows - 1 : rows, :]
        row_out[1, pl.ds(level, 1), :] = field[0:1, :]
        first = jnp.where(lane == level, field[:, 0:1], first)
        last = jnp.where(lane == level, field[:, cols - 1 : cols], last)
        return first, last

    blank = jnp.zeros((rows, LANES), f32)
    first, last = lax.fori_loop(0, levels, pack, (blank, blank))
    for spare in range(levels, row_out.shape[1]):
        for k in range(2):
            row_out[k, spare : spare + 1, :] = jnp.zeros((1, cols), f32)
    col_out[0] = last
    col_out[1] = first
    tcopies = []
    for k in range(4):
        out, into = (row_out, row_in) if k < 2 else (col_out, col_in)
        tcopies.append(
            pltpu.make_async_remote_copy(
                src_ref=out.at[k % 2],
                dst_ref=into.at[k % 2],
                send_sem=tsend_sem.at[k],
                recv_sem=trecv_sem.at[k],
                device_id=side_device(SIDES[k]),
                device_id_type=MESH,
            )
        )
    for copy in tcopies:
        copy.start()
    for copy in copies:
        copy.wait()

    wide, narrow = lax.axis_size("wide"), lax.axis_size("narrow")
    ext_rows, ext_cols = ext.shape[1], ext.shape[2]
    row = iota((ext_rows, ext_cols), 0) + (lax.axis_index("wide") * rows - HR)
    col = iota((ext_rows, ext_cols), 1) + (lax.axis_index("narrow") * cols - HC)
    inside = (row >= 0) & (row < wide * rows) & (col >= 0) & (col < narrow * cols)
    mask = jnp.where(inside, ext[0], 0.0)
    planes_ref[0] = mask
    planes_ref[1] = ext[1]
    planes_ref[2] = ext[2]
    planes_ref[3] = ext[3]

    for slab in range(0, ext_rows, 8):
        at = slice(slab, slab + 8)
        codes = [ext[4 + e, at, :] for e in range(entries)]
        weights = [ext[4 + entries + e, at, :] for e in range(entries)]
        for code in range(9):
            total = jnp.where(codes[0] == code, weights[0], 0.0)
            for e in range(1, entries):
                total = total + jnp.where(codes[e] == code, weights[e], 0.0)
            wsum_ref[code, at, :] = total

    middle = (slice(HR, HR + rows), slice(HC, HC + cols))
    k_north, k_south, k_east, k_west = [
        (kappa_mix * mask * turned(mask, shift, axis))[middle]
        for shift, axis in ((-1, 0), (1, 0), (-1, 1), (1, 1))
    ]
    for copy in tcopies:
        copy.wait()
    row = iota((rows, cols), 0)
    col = iota((rows, cols), 1)

    def diffuse(level, _):
        field = tracer_ref[level]
        here = lane == level
        south = jnp.where(row == 0, row_in[0, pl.ds(level, 1), :], turned(field, 1, 0))
        north = jnp.where(row == rows - 1, row_in[1, pl.ds(level, 1), :], turned(field, -1, 0))
        west_edge = jnp.sum(jnp.where(here, col_in[0], 0.0), axis=1, keepdims=True)
        east_edge = jnp.sum(jnp.where(here, col_in[1], 0.0), axis=1, keepdims=True)
        west = jnp.where(col == 0, west_edge, turned(field, 1, 1))
        east = jnp.where(col == cols - 1, east_edge, turned(field, -1, 1))
        tracer_out_ref[level] = field + (
            k_north * (north - field)
            + k_south * (south - field)
            + k_east * (east - field)
            + k_west * (west - field)
        )
        return 0

    lax.fori_loop(0, levels, diffuse, 0)


def barotropic_kernel(
    flux_ref, wsum_ref, planes_ref,
    heat_ref, height_ref, flow_ref,
    own, ext, spread_cols, forcing, send_sem, recv_sem,
):
    nflux, rows, cols = flux_ref.shape
    ext_rows, ext_cols = planes_ref.shape[1], planes_ref.shape[2]
    wide, narrow = lax.axis_size("wide"), lax.axis_size("narrow")
    my_wide, my_narrow = lax.axis_index("wide"), lax.axis_index("narrow")
    own[...] = flux_ref[...]
    ext[:, HR : HR + rows, HC : HC + cols] = own[...]
    greet()
    copies = edge_copies(own, ext, HR, HC, send_sem, recv_sem)
    for copy in copies:
        copy.start()

    source = iota((cols + 2 * HC, ext_cols), 0) - HC + my_narrow * cols
    half = my_narrow * cols - HC // 2 + lax.shift_right_logical(iota((cols + 2 * HC, ext_cols), 1), 1)
    for dc in range(3):
        wanted = jnp.clip(half + (dc - 1), 0, narrow * cols - 1)
        spread_cols[:, dc * ext_cols : (dc + 1) * ext_cols] = (
            (source == wanted).astype(f32).astype(bf16)
        )
    source = iota((ext_rows, rows + 2 * HR), 1) - HR + my_wide * rows
    half = my_wide * rows - HR // 2 + lax.shift_right_logical(iota((ext_rows, rows + 2 * HR), 0), 1)
    spread_rows = jnp.concatenate(
        [
            (source == jnp.clip(half + (dr - 1), 0, wide * rows - 1)).astype(f32).astype(bf16)
            for dr in range(3)
        ],
        axis=0,
    )
    for copy in copies:
        copy.wait()

    stretched = [
        jnp.dot(ext[f].astype(bf16), spread_cols[...], preferred_element_type=f32).astype(bf16)
        for f in range(nflux)
    ]
    for f in range(nflux):
        doubled = jnp.dot(spread_rows, stretched[f], preferred_element_type=f32)
        total = None
        for code in range(9):
            dr, dc = code // 3, code % 3
            part = doubled[
                dr * ext_rows : (dr + 1) * ext_rows, dc * ext_cols : (dc + 1) * ext_cols
            ]
            term = wsum_ref[code] * part
            total = term if total is None else total + term
        forcing[f] = total

    mask = planes_ref[0]
    mask_east = mask * turned(mask, -1, 1)
    mask_north = mask * turned(mask, -1, 0)
    height, flow_u, flow_v = planes_ref[1], planes_ref[2], planes_ref[3]
    fresh = fresh_gain * forcing[1]
    stress_u = wind_gain * forcing[2]
    stress_v = wind_gain * forcing[3]
    for _ in range(NSUB):
        flow_u = mask_east * (flow_u - gravity * (turned(height, -1, 1) - height) + stress_u)
        flow_v = mask_north * (flow_v - gravity * (turned(height, -1, 0) - height) + stress_v)
        spread = (flow_u - turned(flow_u, 1, 1)) + (flow_v - turned(flow_v, 1, 0))
        height = mask * (height - depth_mean * spread + fresh)
    middle = (
        slice(HR, HR + height_ref.shape[0]),
        slice(HC, HC + height_ref.shape[1]),
    )
    heat_ref[...] = (heat_gain * mask * forcing[0])[middle]
    height_ref[...] = height[middle]
    flow_ref[0] = flow_u[middle]
    flow_ref[1] = flow_v[middle]


def params(**more):
    return pltpu.CompilerParams(vmem_limit_bytes=VMEM_BYTES, **more)


def per_device(
    atm_state,
    group_owner,
    regime_ops,
    flux_map,
    remap_src,
    remap_weight,
    ocean_mask,
    tracer,
    surface_height,
    transports,
):
    peers = lax.axis_size(("wide", "narrow"))
    features, columns_here = atm_state.shape
    nflux = flux_map.shape[1]
    capacity = 2 * columns_here // peers
    total_slots = peers * capacity
    sweeps = regime_ops.shape[1]
    tail = features - LANES
    entries, rows, cols = remap_src.shape
    levels = tracer.shape[0]
    shape = jax.ShapeDtypeStruct

    turned_ops = jnp.swapaxes(regime_ops[0], 1, 2)
    heads = turned_ops[:, :, :LANES].reshape(sweeps * features, LANES)
    rests = jnp.swapaxes(turned_ops[:, :, LANES:], 0, 1).reshape(features, sweeps * tail)
    rests = jnp.pad(rests, ((0, 0), (0, LANES - sweeps * tail)))
    packed = jnp.concatenate([heads, rests], axis=0)
    packed_rows = packed.shape[0]
    gathered = lax.all_gather(packed, ("wide", "narrow"), axis=0, tiled=True)

    placed, slots = pl.pallas_call(
        functools.partial(place_kernel, peers, capacity),
        out_shape=(shape((features, total_slots), bf16), shape((1, columns_here), i32)),
        in_specs=[VMEM] * 2,
        out_specs=(VMEM,) * 2,
        compiler_params=params(),
        cost_estimate=pl.CostEstimate(
            flops=2 * features * columns_here * total_slots,
            bytes_accessed=4 * features * columns_here + 2 * features * total_slots,
            transcendentals=0,
        ),
        name="place",
    )(group_owner.reshape(1, columns_here), atm_state)

    ext_rows, ext_cols = rows + 2 * HR, cols + 2 * HC
    padded_levels = -(-levels // 8) * 8
    wsum, planes, tracer_mixed = pl.pallas_call(
        static_kernel,
        out_shape=(
            shape((9, ext_rows, ext_cols), f32),
            shape((4, ext_rows, ext_cols), f32),
            shape(tracer.shape, f32),
        ),
        in_specs=[VMEM] * 6,
        out_specs=(VMEM,) * 3,
        scratch_shapes=[
            pltpu.VMEM((4 + 2 * entries, rows, cols), f32),
            pltpu.VMEM((4 + 2 * entries, ext_rows, ext_cols), f32),
            pltpu.VMEM((2, padded_levels, cols), f32),
            pltpu.VMEM((2, padded_levels, cols), f32),
            pltpu.VMEM((2, rows, LANES), f32),
            pltpu.VMEM((2, rows, LANES), f32),
            pltpu.SemaphoreType.DMA((8,)),
            pltpu.SemaphoreType.DMA((8,)),
            pltpu.SemaphoreType.DMA((4,)),
            pltpu.SemaphoreType.DMA((4,)),
        ],
        compiler_params=params(collective_id=0, has_side_effects=True),
        cost_estimate=pl.CostEstimate(
            flops=20 * tracer.size, bytes_accessed=8 * tracer.size, transcendentals=0
        ),
        name="static",
    )(remap_src, remap_weight, ocean_mask, tracer, surface_height, transports)

    groups = CHUNK // capacity
    padded_map = jnp.pad(flux_map.T, ((0, 16 - nflux), (0, 0)))
    y_rows = features + 16
    answers = pl.pallas_call(
        functools.partial(physics_kernel, sweeps, capacity, packed_rows),
        grid=(total_slots // CHUNK,),
        out_shape=shape((y_rows, total_slots), bf16),
        in_specs=[
            pl.BlockSpec((groups * packed_rows, LANES), lambda i: (i, 0)),
            pl.BlockSpec((features, CHUNK), lambda i: (0, i)),
            pl.BlockSpec((16, features), lambda i: (0, 0)),
        ],
        out_specs=pl.BlockSpec((y_rows, CHUNK), lambda i: (0, i)),
        compiler_params=params(),
        name="physics",
    )(gathered, placed, padded_map)

    atm_new, fluxes = pl.pallas_call(
        fetch_kernel,
        grid=(columns_here // CHUNK,),
        out_shape=(shape((features, columns_here), f32), shape((16, columns_here), f32)),
        in_specs=[
            pl.BlockSpec((y_rows, total_slots), lambda i: (0, 0)),
            pl.BlockSpec((1, CHUNK), lambda i: (0, i)),
            pl.BlockSpec((features, CHUNK), lambda i: (0, i)),
        ],
        out_specs=(
            pl.BlockSpec((features, CHUNK), lambda i: (0, i)),
            pl.BlockSpec((16, CHUNK), lambda i: (0, i)),
        ),
        compiler_params=params(),
        name="fetch",
    )(answers, slots, atm_state)

    block_rows = columns_here // AC
    flux_block = fluxes[:nflux].reshape(nflux, block_rows, AC)
    heat, height, flows = pl.pallas_call(
        barotropic_kernel,
        out_shape=(
            shape((rows, cols), f32),
            shape((rows, cols), f32),
            shape((2, rows, cols), f32),
        ),
        in_specs=[VMEM] * 3,
        out_specs=(VMEM,) * 3,
        scratch_shapes=[
            pltpu.VMEM((nflux, block_rows, AC), f32),
            pltpu.VMEM((nflux, block_rows + 2 * HR, AC + 2 * HC), f32),
            pltpu.VMEM((AC + 2 * HC, 3 * ext_cols), bf16),
            pltpu.VMEM((nflux, ext_rows, ext_cols), f32),
            pltpu.SemaphoreType.DMA((8,)),
            pltpu.SemaphoreType.DMA((8,)),
        ],
        compiler_params=params(collective_id=1, has_side_effects=True),
        name="barotropic",
    )(flux_block, wsum, planes)
    tracer_new = tracer_mixed.at[0].add(heat)
    return (atm_new, tracer_new, height, flows)


def solution(mesh):
    in_specs = (
        P(None, ("wide", "narrow")),
        P(("wide", "narrow"), None),
        P(("wide", "narrow"), None, None, None),
        P(),
        P(None, "wide", "narrow"),
        P(None, "wide", "narrow"),
        P("wide", "narrow"),
        P(None, "wide", "narrow"),
        P("wide", "narrow"),
        P(None, "wide", "narrow"),
    )
    out_specs = (
        P(None, ("wide", "narrow")),
        P(None, "wide", "narrow"),
        P("wide", "narrow"),
        P(None, "wide", "narrow"),
    )
    return jax.shard_map(
        per_device, mesh=mesh, in_specs=in_specs, out_specs=out_specs, check_vma=False
    )
```

```python
import functools

import jax
import jax.numpy as jnp
from jax import lax
from jax.experimental import pallas as pl
from jax.experimental.pallas import tpu as pltpu
from jax.sharding import PartitionSpec as P

AC = 128
PHYS = 512
NSUB = 4
LANES = 128
CHUNK = 512
VMEM_BYTES = 48 * 1024 * 1024

relax_rate = 0.5
kappa_mix = 0.2
heat_gain = 0.5
gravity = 0.7
depth_mean = 0.7
wind_gain = 0.3
fresh_gain = 0.3

f32 = jnp.float32
bf16 = jnp.bfloat16
i32 = jnp.int32
MESH = pl.DeviceIdType.MESH
SIDES = ((1, 0), (-1, 0), (0, 1), (0, -1), (1, 1), (1, -1), (-1, 1), (-1, -1))
VMEM = pl.BlockSpec(memory_space=pltpu.VMEM)


def iota(shape, dim):
    return lax.broadcasted_iota(i32, shape, dim)


def physics_kernel(sweeps, capacity, packed_rows, ops_ref, xs_ref, fm_ref, y_ref):
    features = xs_ref.shape[0]
    tail = features - LANES
    groups = PHYS // capacity
    initial = [xs_ref[:, g * capacity : (g + 1) * capacity].astype(f32) for g in range(groups)]
    current = list(initial)
    for sweep in range(sweeps):
        for g in range(groups):
            base = g * packed_rows
            rounded = current[g].astype(bf16)
            parts = [rounded[:LANES]]
            if sweep > 0:
                parts.append(jnp.zeros((sweep * tail, capacity), bf16))
            parts.append(rounded[LANES:])
            parts.append(jnp.zeros((LANES - (sweep + 1) * tail, capacity), bf16))
            operand = jnp.concatenate(parts, axis=0)
            head = ops_ref[base + sweep * features : base + (sweep + 1) * features, :]
            rest = ops_ref[base + sweeps * features : base + (sweeps + 1) * features, :]
            matrix = jnp.concatenate([head, rest], axis=1)
            mixed = jnp.dot(matrix, operand, preferred_element_type=f32)
            current[g] = current[g] + relax_rate * jnp.tanh(mixed)
    for g in range(groups):
        cols = slice(g * capacity, (g + 1) * capacity)
        y_ref[:features, cols] = (current[g] - initial[g]).astype(bf16)
        fluxes = jnp.dot(fm_ref[...], current[g].astype(bf16), preferred_element_type=f32)
        y_ref[features:, cols] = fluxes.astype(bf16)


def fetch_kernel(y_ref, slot_ref, atm_ref, new_ref, flux_ref):
    features = atm_ref.shape[0]
    slots = y_ref.shape[1]
    selector = (iota((slots, slot_ref.shape[1]), 0) == slot_ref[...]).astype(f32).astype(bf16)
    returned = jnp.dot(y_ref[...], selector, preferred_element_type=f32)
    new_ref[...] = atm_ref[...] + returned[:features]
    flux_ref[...] = returned[features:]


def side_device(side):
    wide, narrow = lax.axis_size("wide"), lax.axis_size("narrow")
    return (
        lax.rem(lax.axis_index("wide") + side[0] + wide, wide),
        lax.rem(lax.axis_index("narrow") + side[1] + narrow, narrow),
    )


def greet(sides=SIDES):
    barrier = pltpu.get_barrier_semaphore()
    for side in sides:
        pl.semaphore_signal(barrier, inc=1, device_id=side_device(side), device_id_type=MESH)
    pl.semaphore_wait(barrier, len(sides))


def leaving(step, size, halo):
    if step > 0:
        return pl.ds(size - halo, halo)
    return pl.ds(0, halo) if step < 0 else pl.ds(0, size)


def landing(step, size, halo):
    if step > 0:
        return pl.ds(0, halo)
    return pl.ds(halo + size, halo) if step < 0 else pl.ds(halo, size)


def edge_copies(src, dst, halo_rows, halo_cols, send_sem, recv_sem):
    rows, cols = src.shape[1], src.shape[2]
    return [
        pltpu.make_async_remote_copy(
            src_ref=src.at[:, leaving(dr, rows, halo_rows), leaving(dc, cols, halo_cols)],
            dst_ref=dst.at[:, landing(dr, rows, halo_rows), landing(dc, cols, halo_cols)],
            send_sem=send_sem.at[k],
            recv_sem=recv_sem.at[k],
            device_id=side_device((dr, dc)),
            device_id_type=MESH,
        )
        for k, (dr, dc) in enumerate(SIDES)
    ]


HR = 8
HC = 128


def turned(x, shift, axis):
    return pltpu.roll(x, shift % x.shape[axis], axis)


class Gather:
    def __init__(self, packed, slots, send_sem, recv_sem):
        self.packed, self.slots = packed, slots
        self.send_sem, self.recv_sem = send_sem, recv_sem
        wide, self.narrow = lax.axis_size("wide"), lax.axis_size("narrow")
        self.zs = wide // 2
        w, n = lax.axis_index("wide"), lax.axis_index("narrow")
        self.z, self.y, self.x, self.c = w // 2, lax.rem(w, 2), n // 2, lax.rem(n, 2)
        self.offsets = [0]
        for d in range(1, self.zs // 2 + 1):
            self.offsets += [-d, d] if d < self.zs - d else [-d]
        self.sent = {}

    def index(self, kind, k):
        z = lax.rem(self.z + self.offsets[k] + self.zs, self.zs)
        y = 1 - self.y if kind in "yd" else self.y
        x = 1 - self.x if kind in "xd" else self.x
        return (z * 2 + y) * self.narrow + x * 2 + self.c

    def place(self, way):
        z = lax.rem(self.z + way.get("z", 0) + self.zs, self.zs)
        y = 1 - self.y if "y" in way else self.y
        x = 1 - self.x if "x" in way else self.x
        c = 1 - self.c if "c" in way else self.c
        return z * 2 + y, x * 2 + c

    def number(self, kind, k):
        if kind[0] == "c":
            return 4 * self.zs + self.number(kind[1], k)
        return "zxyd".index(kind) * self.zs + k

    def send(self, have, k, kind, to, way):
        at = self.index(have, k)
        event = self.number(kind, to)
        copy = pltpu.make_async_remote_copy(
            src_ref=self.packed if have == "z" and k == 0 else self.slots.at[at],
            dst_ref=self.slots.at[at],
            send_sem=self.send_sem.at[event],
            recv_sem=self.recv_sem.at[event],
            device_id=self.place(way),
            device_id_type=MESH,
        )
        copy.start()
        self.sent[kind, to] = copy

    def onward(self, kind, k):
        if kind == "z":
            d = self.offsets[k]
            if d <= 0 and d - 1 in self.offsets:
                self.send("z", k, "z", self.offsets.index(d - 1), {"z": 1})
            if d >= 0 and d + 1 in self.offsets:
                self.send("z", k, "z", self.offsets.index(d + 1), {"z": -1})
            self.send("z", k, "x", k, {"x": 1})
            self.send("z", k, "y", k, {"y": 1})
        elif kind == "x" and k % 2 == 0:
            self.send("x", k, "d", k, {"y": 1})
        elif kind == "y" and k % 2 == 1:
            self.send("y", k, "d", k, {"x": 1})
        self.send(kind, k, "c" + kind, k, {"c": 1})

    def arrive(self, kind, k):
        self.sent[kind, k].wait_recv()
        if kind[0] != "c":
            self.onward(kind, k)

    def rounds(self):
        steps = []
        for k in range(self.zs):
            if k > 0:
                steps.append([("z", k)])
                steps.append([("x", k - 1), ("y", k - 1)])
        steps.append([("x", self.zs - 1), ("y", self.zs - 1)])
        for k in range(self.zs):
            steps.append([("d", k)])
        return steps


AROUND = SIDES + ((2, 0), (-2, 0), (0, 2))


def prepare_kernel(
    capacity,
    packed_hbm, owner_ref, atm_hbm, src_hbm, weight_hbm, mask_hbm, tracer_hbm, height_hbm, flow_hbm,
    slots_hbm, xs_ref, slot_ref, wsum_ref, planes_ref, tracer_out_ref,
    atm_ref, src_ref, weight_ref, mask_ref, tracer_ref, height_ref, flow_ref,
    own, ext, row_out, row_in, col_out, col_in, coef,
    gsend_sem, grecv_sem, load_sem, send_sem, recv_sem, tsend_sem, trecv_sem,
):
    entries, rows, cols = src_ref.shape
    levels = tracer_ref.shape[0]
    wide, narrow = lax.axis_size("wide"), lax.axis_size("narrow")
    peers = wide * narrow
    gather = Gather(packed_hbm, slots_hbm, gsend_sem, grecv_sem)
    loads = [
        pltpu.make_async_copy(a, b, load_sem.at[k])
        for k, (a, b) in enumerate(
            (
                (mask_hbm, mask_ref),
                (height_hbm, height_ref),
                (flow_hbm, flow_ref),
                (src_hbm, src_ref),
                (weight_hbm, weight_ref),
                (tracer_hbm, tracer_ref),
                (atm_hbm, atm_ref),
                (packed_hbm, slots_hbm.at[gather.index("z", 0)]),
            )
        )
    ]
    for load in loads:
        load.start()
    greet(AROUND)
    gather.onward("z", 0)

    for load in loads[:5]:
        load.wait()
    own[0] = mask_ref[...].astype(f32)
    own[1] = height_ref[...]
    own[2] = flow_ref[0]
    own[3] = flow_ref[1]
    for e in range(entries):
        own[4 + e] = src_ref[e].astype(f32)
        own[4 + entries + e] = weight_ref[e]
    ext[:, HR : HR + rows, HC : HC + cols] = own[...]
    copies = edge_copies(own, ext, HR, HC, send_sem, recv_sem)
    for copy in copies:
        copy.start()
    loads[5].wait()

    lane = iota((rows, LANES), 1)

    def pack(level, carry):
        first, last = carry
        field = tracer_ref[level]
        row_out[0, pl.ds(level, 1), :] = field[rows - 1 : rows, :]
        row_out[1, pl.ds(level, 1), :] = field[0:1, :]
        first = jnp.where(lane == level, field[:, 0:1], first)
        last = jnp.where(lane == level, field[:, cols - 1 : cols], last)
        return first, last

    blank = jnp.zeros((rows, LANES), f32)
    first, last = lax.fori_loop(0, levels, pack, (blank, blank))
    for spare in range(levels, row_out.shape[1]):
        for k in range(2):
            row_out[k, spare : spare + 1, :] = jnp.zeros((1, cols), f32)
    col_out[0] = last
    col_out[1] = first
    tcopies = []
    for k in range(4):
        out, into = (row_out, row_in) if k < 2 else (col_out, col_in)
        tcopies.append(
            pltpu.make_async_remote_copy(
                src_ref=out.at[k % 2],
                dst_ref=into.at[k % 2],
                send_sem=tsend_sem.at[k],
                recv_sem=trecv_sem.at[k],
                device_id=side_device(SIDES[k]),
                device_id_type=MESH,
            )
        )
    for copy in tcopies:
        copy.start()

    def rank():
        loads[6].wait()
        loads[7].wait()
        count = owner_ref.shape[1]
        upper = (iota((LANES, LANES), 0) < iota((LANES, LANES), 1)).astype(f32).astype(bf16)
        ids = iota((peers, LANES), 0)
        carry = jnp.zeros((peers, 1), f32)
        for start in range(0, count, LANES):
            owner = owner_ref[:, start : start + LANES]
            hot = (ids == owner).astype(f32)
            before = jnp.dot(hot.astype(bf16), upper, preferred_element_type=f32) + carry
            ranks = jnp.sum(hot * before, axis=0, keepdims=True)
            slot_ref[:, start : start + LANES] = owner * capacity + ranks.astype(i32)
            carry = carry + jnp.sum(hot, axis=1, keepdims=True)

    def place(first, last):
        columns = atm_ref[...].astype(bf16)

        def step(i, _):
            begin = pl.multiple_of(i * CHUNK, CHUNK)
            selector = (iota((CHUNK, slot_ref.shape[1]), 0) + begin == slot_ref[...]).astype(f32)
            placed = lax.dot_general(
                columns, selector.astype(bf16), (((1,), (1,)), ((), ())), preferred_element_type=f32
            )
            xs_ref[:, pl.ds(begin, CHUNK)] = placed.astype(bf16)
            return 0

        lax.fori_loop(first, last, step, 0)

    middle = (slice(HR, HR + rows), slice(HC, HC + cols))
    ext_rows, ext_cols = ext.shape[1], ext.shape[2]

    def planes():
        for copy in copies:
            copy.wait()
        row = iota((ext_rows, ext_cols), 0) + (lax.axis_index("wide") * rows - HR)
        col = iota((ext_rows, ext_cols), 1) + (lax.axis_index("narrow") * cols - HC)
        inside = (row >= 0) & (row < wide * rows) & (col >= 0) & (col < narrow * cols)
        mask = jnp.where(inside, ext[0], 0.0)
        planes_ref[0] = mask
        planes_ref[1] = ext[1]
        planes_ref[2] = ext[2]
        planes_ref[3] = ext[3]
        for k, (shift, axis) in enumerate(((-1, 0), (1, 0), (-1, 1), (1, 1))):
            coef[k] = (kappa_mix * mask * turned(mask, shift, axis))[middle]

    def weights(first, last):
        for slab in range(first, last, 8):
            at = slice(slab, slab + 8)
            codes = [ext[4 + e, at, :] for e in range(entries)]
            parts = [ext[4 + entries + e, at, :] for e in range(entries)]
            for code in range(9):
                total = jnp.where(codes[0] == code, parts[0], 0.0)
                for e in range(1, entries):
                    total = total + jnp.where(codes[e] == code, parts[e], 0.0)
                wsum_ref[code, at, :] = total

    row = iota((rows, cols), 0)
    col = iota((rows, cols), 1)

    def diffuse(level, _):
        field = tracer_ref[level]
        here = lane == level
        south = jnp.where(row == 0, row_in[0, pl.ds(level, 1), :], turned(field, 1, 0))
        north = jnp.where(row == rows - 1, row_in[1, pl.ds(level, 1), :], turned(field, -1, 0))
        west_edge = jnp.sum(jnp.where(here, col_in[0], 0.0), axis=1, keepdims=True)
        east_edge = jnp.sum(jnp.where(here, col_in[1], 0.0), axis=1, keepdims=True)
        west = jnp.where(col == 0, west_edge, turned(field, 1, 1))
        east = jnp.where(col == cols - 1, east_edge, turned(field, -1, 1))
        tracer_out_ref[level] = field + (
            coef[0] * (north - field)
            + coef[1] * (south - field)
            + coef[2] * (east - field)
            + coef[3] * (west - field)
        )
        return 0

    def mix(first, last):
        if first == 0:
            for copy in tcopies:
                copy.wait()
        lax.fori_loop(first, last, diffuse, 0)

    chunks = xs_ref.shape[1] // CHUNK
    work = [rank]
    work += [functools.partial(place, i, min(i + 2, chunks)) for i in range(0, chunks, 2)]
    work += [planes]
    work += [functools.partial(weights, i, i + 16) for i in range(0, ext_rows, 16)]
    work += [functools.partial(mix, i, min(i + 16, levels)) for i in range(0, levels, 16)]
    for events in gather.rounds():
        if work:
            work.pop(0)()
        for event in events:
            gather.arrive(*event)
    while work:
        work.pop(0)()
    for kind in "zxyd":
        for k in range(gather.zs):
            gather.arrive("c" + kind, k)
    for copy in gather.sent.values():
        copy.wait_send()


def barotropic_kernel(
    flux_ref, wsum_ref, planes_ref,
    heat_ref, height_ref, flow_ref,
    own, ext, spread_cols, forcing, send_sem, recv_sem,
):
    nflux, rows, cols = flux_ref.shape
    ext_rows, ext_cols = planes_ref.shape[1], planes_ref.shape[2]
    wide, narrow = lax.axis_size("wide"), lax.axis_size("narrow")
    my_wide, my_narrow = lax.axis_index("wide"), lax.axis_index("narrow")
    own[...] = flux_ref[...]
    ext[:, HR : HR + rows, HC : HC + cols] = own[...]
    greet()
    copies = edge_copies(own, ext, HR, HC, send_sem, recv_sem)
    for copy in copies:
        copy.start()

    source = iota((cols + 2 * HC, ext_cols), 0) - HC + my_narrow * cols
    half = my_narrow * cols - HC // 2 + lax.shift_right_logical(iota((cols + 2 * HC, ext_cols), 1), 1)
    for dc in range(3):
        wanted = jnp.clip(half + (dc - 1), 0, narrow * cols - 1)
        spread_cols[:, dc * ext_cols : (dc + 1) * ext_cols] = (
            (source == wanted).astype(f32).astype(bf16)
        )
    source = iota((ext_rows, rows + 2 * HR), 1) - HR + my_wide * rows
    half = my_wide * rows - HR // 2 + lax.shift_right_logical(iota((ext_rows, rows + 2 * HR), 0), 1)
    spread_rows = jnp.concatenate(
        [
            (source == jnp.clip(half + (dr - 1), 0, wide * rows - 1)).astype(f32).astype(bf16)
            for dr in range(3)
        ],
        axis=0,
    )
    for copy in copies:
        copy.wait()

    stretched = [
        jnp.dot(ext[f].astype(bf16), spread_cols[...], preferred_element_type=f32).astype(bf16)
        for f in range(nflux)
    ]
    for f in range(nflux):
        doubled = jnp.dot(spread_rows, stretched[f], preferred_element_type=f32)
        total = None
        for code in range(9):
            dr, dc = code // 3, code % 3
            part = doubled[
                dr * ext_rows : (dr + 1) * ext_rows, dc * ext_cols : (dc + 1) * ext_cols
            ]
            term = wsum_ref[code] * part
            total = term if total is None else total + term
        forcing[f] = total

    mask = planes_ref[0]
    mask_east = mask * turned(mask, -1, 1)
    mask_north = mask * turned(mask, -1, 0)
    height, flow_u, flow_v = planes_ref[1], planes_ref[2], planes_ref[3]
    fresh = fresh_gain * forcing[1]
    stress_u = wind_gain * forcing[2]
    stress_v = wind_gain * forcing[3]
    for _ in range(NSUB):
        flow_u = mask_east * (flow_u - gravity * (turned(height, -1, 1) - height) + stress_u)
        flow_v = mask_north * (flow_v - gravity * (turned(height, -1, 0) - height) + stress_v)
        spread = (flow_u - turned(flow_u, 1, 1)) + (flow_v - turned(flow_v, 1, 0))
        height = mask * (height - depth_mean * spread + fresh)
    middle = (
        slice(HR, HR + height_ref.shape[0]),
        slice(HC, HC + height_ref.shape[1]),
    )
    heat_ref[...] = (heat_gain * mask * forcing[0])[middle]
    height_ref[...] = height[middle]
    flow_ref[0] = flow_u[middle]
    flow_ref[1] = flow_v[middle]


def params(**more):
    return pltpu.CompilerParams(vmem_limit_bytes=VMEM_BYTES, **more)


def per_device(
    atm_state,
    group_owner,
    regime_ops,
    flux_map,
    remap_src,
    remap_weight,
    ocean_mask,
    tracer,
    surface_height,
    transports,
):
    peers = lax.axis_size(("wide", "narrow"))
    features, columns_here = atm_state.shape
    nflux = flux_map.shape[1]
    capacity = 2 * columns_here // peers
    total_slots = peers * capacity
    sweeps = regime_ops.shape[1]
    tail = features - LANES
    entries, rows, cols = remap_src.shape
    levels = tracer.shape[0]
    shape = jax.ShapeDtypeStruct

    turned_ops = jnp.swapaxes(regime_ops[0], 1, 2)
    heads = turned_ops[:, :, :LANES].reshape(sweeps * features, LANES)
    rests = jnp.swapaxes(turned_ops[:, :, LANES:], 0, 1).reshape(features, sweeps * tail)
    rests = jnp.pad(rests, ((0, 0), (0, LANES - sweeps * tail)))
    packed = jnp.concatenate([heads, rests], axis=0)
    packed_rows = packed.shape[0]
    ext_rows, ext_cols = rows + 2 * HR, cols + 2 * HC
    padded_levels = -(-levels // 8) * 8
    gather_events = 8 * (lax.axis_size("wide") // 2)
    hbm = pl.BlockSpec(memory_space=pl.ANY)
    gathered, placed, slots, wsum, planes, tracer_mixed = pl.pallas_call(
        functools.partial(prepare_kernel, capacity),
        out_shape=(
            shape((peers,) + packed.shape, bf16),
            shape((features, total_slots), bf16),
            shape((1, columns_here), i32),
            shape((9, ext_rows, ext_cols), f32),
            shape((4, ext_rows, ext_cols), f32),
            shape(tracer.shape, f32),
        ),
        in_specs=[hbm, VMEM] + [hbm] * 7,
        out_specs=(hbm,) + (VMEM,) * 5,
        scratch_shapes=[
            pltpu.VMEM(atm_state.shape, f32),
            pltpu.VMEM(remap_src.shape, i32),
            pltpu.VMEM(remap_weight.shape, f32),
            pltpu.VMEM(ocean_mask.shape, i32),
            pltpu.VMEM(tracer.shape, f32),
            pltpu.VMEM(surface_height.shape, f32),
            pltpu.VMEM(transports.shape, f32),
            pltpu.VMEM((4 + 2 * entries, rows, cols), f32),
            pltpu.VMEM((4 + 2 * entries, ext_rows, ext_cols), f32),
            pltpu.VMEM((2, padded_levels, cols), f32),
            pltpu.VMEM((2, padded_levels, cols), f32),
            pltpu.VMEM((2, rows, LANES), f32),
            pltpu.VMEM((2, rows, LANES), f32),
            pltpu.VMEM((4, rows, cols), f32),
            pltpu.SemaphoreType.DMA((gather_events,)),
            pltpu.SemaphoreType.DMA((gather_events,)),
            pltpu.SemaphoreType.DMA((8,)),
            pltpu.SemaphoreType.DMA((8,)),
            pltpu.SemaphoreType.DMA((8,)),
            pltpu.SemaphoreType.DMA((4,)),
            pltpu.SemaphoreType.DMA((4,)),
        ],
        compiler_params=params(collective_id=0, has_side_effects=True),
        cost_estimate=pl.CostEstimate(
            flops=2 * features * columns_here * total_slots,
            bytes_accessed=8 * tracer.size,
            transcendentals=0,
        ),
        name="prepare",
    )(
        packed,
        group_owner.reshape(1, columns_here),
        atm_state,
        remap_src,
        remap_weight,
        ocean_mask,
        tracer,
        surface_height,
        transports,
    )
    gathered = gathered.reshape(peers * packed_rows, LANES)

    groups = PHYS // capacity
    padded_map = jnp.pad(flux_map.T, ((0, 16 - nflux), (0, 0)))
    y_rows = features + 16
    answers = pl.pallas_call(
        functools.partial(physics_kernel, sweeps, capacity, packed_rows),
        grid=(total_slots // PHYS,),
        out_shape=shape((y_rows, total_slots), bf16),
        in_specs=[
            pl.BlockSpec((groups * packed_rows, LANES), lambda i: (i, 0)),
            pl.BlockSpec((features, PHYS), lambda i: (0, i)),
            pl.BlockSpec((16, features), lambda i: (0, 0)),
        ],
        out_specs=pl.BlockSpec((y_rows, PHYS), lambda i: (0, i)),
        compiler_params=params(),
        name="physics",
    )(gathered, placed, padded_map)

    atm_new, fluxes = pl.pallas_call(
        fetch_kernel,
        grid=(columns_here // CHUNK,),
        out_shape=(shape((features, columns_here), f32), shape((16, columns_here), f32)),
        in_specs=[
            pl.BlockSpec((y_rows, total_slots), lambda i: (0, 0)),
            pl.BlockSpec((1, CHUNK), lambda i: (0, i)),
            pl.BlockSpec((features, CHUNK), lambda i: (0, i)),
        ],
        out_specs=(
            pl.BlockSpec((features, CHUNK), lambda i: (0, i)),
            pl.BlockSpec((16, CHUNK), lambda i: (0, i)),
        ),
        compiler_params=params(),
        name="fetch",
    )(answers, slots, atm_state)

    block_rows = columns_here // AC
    flux_block = fluxes[:nflux].reshape(nflux, block_rows, AC)
    heat, height, flows = pl.pallas_call(
        barotropic_kernel,
        out_shape=(
            shape((rows, cols), f32),
            shape((rows, cols), f32),
            shape((2, rows, cols), f32),
        ),
        in_specs=[VMEM] * 3,
        out_specs=(VMEM,) * 3,
        scratch_shapes=[
            pltpu.VMEM((nflux, block_rows, AC), f32),
            pltpu.VMEM((nflux, block_rows + 2 * HR, AC + 2 * HC), f32),
            pltpu.VMEM((AC + 2 * HC, 3 * ext_cols), bf16),
            pltpu.VMEM((nflux, ext_rows, ext_cols), f32),
            pltpu.SemaphoreType.DMA((8,)),
            pltpu.SemaphoreType.DMA((8,)),
        ],
        compiler_params=params(collective_id=1, has_side_effects=True),
        name="barotropic",
    )(flux_block, wsum, planes)
    tracer_new = tracer_mixed.at[0].add(heat)
    return (atm_new, tracer_new, height, flows)


def solution(mesh):
    in_specs = (
        P(None, ("wide", "narrow")),
        P(("wide", "narrow"), None),
        P(("wide", "narrow"), None, None, None),
        P(),
        P(None, "wide", "narrow"),
        P(None, "wide", "narrow"),
        P("wide", "narrow"),
        P(None, "wide", "narrow"),
        P("wide", "narrow"),
        P(None, "wide", "narrow"),
    )
    out_specs = (
        P(None, ("wide", "narrow")),
        P(None, "wide", "narrow"),
        P("wide", "narrow"),
        P(None, "wide", "narrow"),
    )
    return jax.shard_map(
        per_device, mesh=mesh, in_specs=in_specs, out_specs=out_specs, check_vma=False
    )
```

```python
import functools

import jax
import jax.numpy as jnp
from jax import lax
from jax.experimental import pallas as pl
from jax.experimental.pallas import tpu as pltpu
from jax.sharding import PartitionSpec as P

AC = 128
PHYS = 512
NSUB = 4
LANES = 128
CHUNK = 512
VMEM_BYTES = 48 * 1024 * 1024
ALL_VMEM_BYTES = 60 * 1024 * 1024

relax_rate = 0.5
kappa_mix = 0.2
heat_gain = 0.5
gravity = 0.7
depth_mean = 0.7
wind_gain = 0.3
fresh_gain = 0.3

f32 = jnp.float32
bf16 = jnp.bfloat16
i32 = jnp.int32
MESH = pl.DeviceIdType.MESH
SIDES = ((1, 0), (-1, 0), (0, 1), (0, -1), (1, 1), (1, -1), (-1, 1), (-1, -1))
VMEM = pl.BlockSpec(memory_space=pltpu.VMEM)


def iota(shape, dim):
    return lax.broadcasted_iota(i32, shape, dim)


def physics_kernel(sweeps, capacity, packed_rows, ops_ref, xs_ref, fm_ref, y_ref):
    features = xs_ref.shape[0]
    tail = features - LANES
    groups = PHYS // capacity
    initial = [xs_ref[:, g * capacity : (g + 1) * capacity].astype(f32) for g in range(groups)]
    current = list(initial)
    for sweep in range(sweeps):
        for g in range(groups):
            base = g * packed_rows
            rounded = current[g].astype(bf16)
            parts = [rounded[:LANES]]
            if sweep > 0:
                parts.append(jnp.zeros((sweep * tail, capacity), bf16))
            parts.append(rounded[LANES:])
            parts.append(jnp.zeros((LANES - (sweep + 1) * tail, capacity), bf16))
            operand = jnp.concatenate(parts, axis=0)
            head = ops_ref[base + sweep * features : base + (sweep + 1) * features, :]
            rest = ops_ref[base + sweeps * features : base + (sweeps + 1) * features, :]
            matrix = jnp.concatenate([head, rest], axis=1)
            mixed = jnp.dot(matrix, operand, preferred_element_type=f32)
            current[g] = current[g] + relax_rate * jnp.tanh(mixed)
    for g in range(groups):
        cols = slice(g * capacity, (g + 1) * capacity)
        y_ref[:features, cols] = (current[g] - initial[g]).astype(bf16)
        fluxes = jnp.dot(fm_ref[...], current[g].astype(bf16), preferred_element_type=f32)
        y_ref[features:, cols] = fluxes.astype(bf16)


def fetch_kernel(y_ref, slot_ref, atm_ref, new_ref, flux_ref):
    features = atm_ref.shape[0]
    slots = y_ref.shape[1]
    selector = (iota((slots, slot_ref.shape[1]), 0) == slot_ref[...]).astype(f32).astype(bf16)
    returned = jnp.dot(y_ref[...], selector, preferred_element_type=f32)
    new_ref[...] = atm_ref[...] + returned[:features]
    flux_ref[...] = returned[features:]


def side_device(side):
    wide, narrow = lax.axis_size("wide"), lax.axis_size("narrow")
    return (
        lax.rem(lax.axis_index("wide") + side[0] + wide, wide),
        lax.rem(lax.axis_index("narrow") + side[1] + narrow, narrow),
    )


def greet(sides=SIDES):
    barrier = pltpu.get_barrier_semaphore()
    for side in sides:
        pl.semaphore_signal(barrier, inc=1, device_id=side_device(side), device_id_type=MESH)
    pl.semaphore_wait(barrier, len(sides))


def leaving(step, size, halo):
    if step > 0:
        return pl.ds(size - halo, halo)
    return pl.ds(0, halo) if step < 0 else pl.ds(0, size)


def landing(step, size, halo):
    if step > 0:
        return pl.ds(0, halo)
    return pl.ds(halo + size, halo) if step < 0 else pl.ds(halo, size)


def edge_copies(src, dst, halo_rows, halo_cols, send_sem, recv_sem):
    rows, cols = src.shape[1], src.shape[2]
    return [
        pltpu.make_async_remote_copy(
            src_ref=src.at[:, leaving(dr, rows, halo_rows), leaving(dc, cols, halo_cols)],
            dst_ref=dst.at[:, landing(dr, rows, halo_rows), landing(dc, cols, halo_cols)],
            send_sem=send_sem.at[k],
            recv_sem=recv_sem.at[k],
            device_id=side_device((dr, dc)),
            device_id_type=MESH,
        )
        for k, (dr, dc) in enumerate(SIDES)
    ]


HR = 8
HC = 128


def turned(x, shift, axis):
    return pltpu.roll(x, shift % x.shape[axis], axis)


class Gather:
    def __init__(self, packed, slots, send_sem, recv_sem):
        self.packed, self.slots = packed, slots
        self.send_sem, self.recv_sem = send_sem, recv_sem
        wide, self.narrow = lax.axis_size("wide"), lax.axis_size("narrow")
        self.zs = wide // 2
        w, n = lax.axis_index("wide"), lax.axis_index("narrow")
        self.z, self.y, self.x, self.c = w // 2, lax.rem(w, 2), n // 2, lax.rem(n, 2)
        self.offsets = [0]
        for d in range(1, self.zs // 2 + 1):
            self.offsets += [-d, d] if d < self.zs - d else [-d]
        self.sent = {}

    def index(self, kind, k):
        z = lax.rem(self.z + self.offsets[k] + self.zs, self.zs)
        y = 1 - self.y if kind in "yd" else self.y
        x = 1 - self.x if kind in "xd" else self.x
        return (z * 2 + y) * self.narrow + x * 2 + self.c

    def place(self, way):
        z = lax.rem(self.z + way.get("z", 0) + self.zs, self.zs)
        y = 1 - self.y if "y" in way else self.y
        x = 1 - self.x if "x" in way else self.x
        c = 1 - self.c if "c" in way else self.c
        return z * 2 + y, x * 2 + c

    def number(self, kind, k):
        if kind[0] == "c":
            return 4 * self.zs + self.number(kind[1], k)
        return "zxyd".index(kind) * self.zs + k

    def send(self, have, k, kind, to, way):
        at = self.index(have, k)
        event = self.number(kind, to)
        copy = pltpu.make_async_remote_copy(
            src_ref=self.packed if have == "z" and k == 0 else self.slots.at[at],
            dst_ref=self.slots.at[at],
            send_sem=self.send_sem.at[event],
            recv_sem=self.recv_sem.at[event],
            device_id=self.place(way),
            device_id_type=MESH,
        )
        copy.start()
        self.sent[kind, to] = copy

    def onward(self, kind, k):
        if kind == "z":
            d = self.offsets[k]
            if d <= 0 and d - 1 in self.offsets:
                self.send("z", k, "z", self.offsets.index(d - 1), {"z": 1})
            if d >= 0 and d + 1 in self.offsets:
                self.send("z", k, "z", self.offsets.index(d + 1), {"z": -1})
            self.send("z", k, "x", k, {"x": 1})
            self.send("z", k, "y", k, {"y": 1})
        elif kind == "x" and k % 2 == 0:
            self.send("x", k, "d", k, {"y": 1})
        elif kind == "y" and k % 2 == 1:
            self.send("y", k, "d", k, {"x": 1})
        self.send(kind, k, "c" + kind, k, {"c": 1})

    def arrive(self, kind, k):
        self.sent[kind, k].wait_recv()
        if kind[0] != "c":
            self.onward(kind, k)

    def rounds(self):
        steps = []
        for k in range(self.zs):
            if k > 0:
                steps.append([("z", k)])
                steps.append([("x", k - 1), ("y", k - 1)])
        steps.append([("x", self.zs - 1), ("y", self.zs - 1)])
        for k in range(self.zs):
            steps.append([("d", k)])
        return steps


AROUND = SIDES + ((2, 0), (-2, 0), (0, 2))


def prepare_kernel(
    capacity,
    packed_hbm, owner_ref, atm_hbm, src_hbm, weight_hbm, mask_hbm, tracer_hbm, height_hbm, flow_hbm,
    slots_hbm, xs_ref, slot_ref, wsum_ref, planes_ref, tracer_out_ref,
    atm_ref, src_ref, weight_ref, mask_ref, tracer_ref, height_ref, flow_ref,
    own, ext, row_out, row_in, col_out, col_in, coef,
    gsend_sem, grecv_sem, load_sem, send_sem, recv_sem, tsend_sem, trecv_sem,
):
    entries, rows, cols = src_ref.shape
    levels = tracer_ref.shape[0]
    wide, narrow = lax.axis_size("wide"), lax.axis_size("narrow")
    peers = wide * narrow
    gather = Gather(packed_hbm, slots_hbm, gsend_sem, grecv_sem)
    loads = [
        pltpu.make_async_copy(a, b, load_sem.at[k])
        for k, (a, b) in enumerate(
            (
                (mask_hbm, mask_ref),
                (height_hbm, height_ref),
                (flow_hbm, flow_ref),
                (src_hbm, src_ref),
                (weight_hbm, weight_ref),
                (tracer_hbm, tracer_ref),
                (atm_hbm, atm_ref),
                (packed_hbm, slots_hbm.at[gather.index("z", 0)]),
            )
        )
    ]
    for load in loads:
        load.start()
    greet(AROUND)
    gather.onward("z", 0)

    for load in loads[:5]:
        load.wait()
    own[0] = mask_ref[...].astype(f32)
    own[1] = height_ref[...]
    own[2] = flow_ref[0]
    own[3] = flow_ref[1]
    for e in range(entries):
        own[4 + e] = src_ref[e].astype(f32)
        own[4 + entries + e] = weight_ref[e]
    ext[:, HR : HR + rows, HC : HC + cols] = own[...]
    copies = edge_copies(own, ext, HR, HC, send_sem, recv_sem)
    for copy in copies:
        copy.start()
    loads[5].wait()

    lane = iota((rows, LANES), 1)

    def pack(level, carry):
        first, last = carry
        field = tracer_ref[level]
        row_out[0, pl.ds(level, 1), :] = field[rows - 1 : rows, :]
        row_out[1, pl.ds(level, 1), :] = field[0:1, :]
        first = jnp.where(lane == level, field[:, 0:1], first)
        last = jnp.where(lane == level, field[:, cols - 1 : cols], last)
        return first, last

    blank = jnp.zeros((rows, LANES), f32)
    first, last = lax.fori_loop(0, levels, pack, (blank, blank))
    for spare in range(levels, row_out.shape[1]):
        for k in range(2):
            row_out[k, spare : spare + 1, :] = jnp.zeros((1, cols), f32)
    col_out[0] = last
    col_out[1] = first
    tcopies = []
    for k in range(4):
        out, into = (row_out, row_in) if k < 2 else (col_out, col_in)
        tcopies.append(
            pltpu.make_async_remote_copy(
                src_ref=out.at[k % 2],
                dst_ref=into.at[k % 2],
                send_sem=tsend_sem.at[k],
                recv_sem=trecv_sem.at[k],
                device_id=side_device(SIDES[k]),
                device_id_type=MESH,
            )
        )
    for copy in tcopies:
        copy.start()

    def rank():
        loads[6].wait()
        loads[7].wait()
        count = owner_ref.shape[1]
        upper = (iota((LANES, LANES), 0) < iota((LANES, LANES), 1)).astype(f32).astype(bf16)
        ids = iota((peers, LANES), 0)
        carry = jnp.zeros((peers, 1), f32)
        for start in range(0, count, LANES):
            owner = owner_ref[:, start : start + LANES]
            hot = (ids == owner).astype(f32)
            before = jnp.dot(hot.astype(bf16), upper, preferred_element_type=f32) + carry
            ranks = jnp.sum(hot * before, axis=0, keepdims=True)
            slot_ref[:, start : start + LANES] = owner * capacity + ranks.astype(i32)
            carry = carry + jnp.sum(hot, axis=1, keepdims=True)

    def place(first, last):
        columns = atm_ref[...].astype(bf16)

        def step(i, _):
            begin = pl.multiple_of(i * CHUNK, CHUNK)
            selector = (iota((CHUNK, slot_ref.shape[1]), 0) + begin == slot_ref[...]).astype(f32)
            placed = lax.dot_general(
                columns, selector.astype(bf16), (((1,), (1,)), ((), ())), preferred_element_type=f32
            )
            xs_ref[:, pl.ds(begin, CHUNK)] = placed.astype(bf16)
            return 0

        lax.fori_loop(first, last, step, 0)

    middle = (slice(HR, HR + rows), slice(HC, HC + cols))
    ext_rows, ext_cols = ext.shape[1], ext.shape[2]

    def planes():
        for copy in copies:
            copy.wait()
        row = iota((ext_rows, ext_cols), 0) + (lax.axis_index("wide") * rows - HR)
        col = iota((ext_rows, ext_cols), 1) + (lax.axis_index("narrow") * cols - HC)
        inside = (row >= 0) & (row < wide * rows) & (col >= 0) & (col < narrow * cols)
        mask = jnp.where(inside, ext[0], 0.0)
        planes_ref[0] = mask
        planes_ref[1] = ext[1]
        planes_ref[2] = ext[2]
        planes_ref[3] = ext[3]
        for k, (shift, axis) in enumerate(((-1, 0), (1, 0), (-1, 1), (1, 1))):
            coef[k] = (kappa_mix * mask * turned(mask, shift, axis))[middle]

    def weights(first, last):
        for slab in range(first, last, 8):
            at = slice(slab, slab + 8)
            codes = [ext[4 + e, at, :] for e in range(entries)]
            parts = [ext[4 + entries + e, at, :] for e in range(entries)]
            for code in range(9):
                total = jnp.where(codes[0] == code, parts[0], 0.0)
                for e in range(1, entries):
                    total = total + jnp.where(codes[e] == code, parts[e], 0.0)
                wsum_ref[code, at, :] = total

    row = iota((rows, cols), 0)
    col = iota((rows, cols), 1)

    def diffuse(level, _):
        field = tracer_ref[level]
        here = lane == level
        south = jnp.where(row == 0, row_in[0, pl.ds(level, 1), :], turned(field, 1, 0))
        north = jnp.where(row == rows - 1, row_in[1, pl.ds(level, 1), :], turned(field, -1, 0))
        west_edge = jnp.sum(jnp.where(here, col_in[0], 0.0), axis=1, keepdims=True)
        east_edge = jnp.sum(jnp.where(here, col_in[1], 0.0), axis=1, keepdims=True)
        west = jnp.where(col == 0, west_edge, turned(field, 1, 1))
        east = jnp.where(col == cols - 1, east_edge, turned(field, -1, 1))
        tracer_out_ref[level] = field + (
            coef[0] * (north - field)
            + coef[1] * (south - field)
            + coef[2] * (east - field)
            + coef[3] * (west - field)
        )
        return 0

    def mix(first, last):
        if first == 0:
            for copy in tcopies:
                copy.wait()
        lax.fori_loop(first, last, diffuse, 0)

    chunks = xs_ref.shape[1] // CHUNK
    work = [rank]
    work += [functools.partial(place, i, min(i + 2, chunks)) for i in range(0, chunks, 2)]
    work += [planes]
    work += [functools.partial(weights, i, i + 16) for i in range(0, ext_rows, 16)]
    work += [functools.partial(mix, i, min(i + 16, levels)) for i in range(0, levels, 16)]
    for events in gather.rounds():
        if work:
            work.pop(0)()
        for event in events:
            gather.arrive(*event)
    while work:
        work.pop(0)()
    for kind in "zxyd":
        for k in range(gather.zs):
            gather.arrive("c" + kind, k)
    for copy in gather.sent.values():
        copy.wait_send()


def barotropic_kernel(
    flux_ref, wsum_ref, planes_ref,
    heat_ref, height_ref, flow_ref,
    own, ext, spread_cols, forcing, send_sem, recv_sem,
):
    nflux, rows, cols = flux_ref.shape
    ext_rows, ext_cols = planes_ref.shape[1], planes_ref.shape[2]
    wide, narrow = lax.axis_size("wide"), lax.axis_size("narrow")
    my_wide, my_narrow = lax.axis_index("wide"), lax.axis_index("narrow")
    own[...] = flux_ref[...]
    ext[:, HR : HR + rows, HC : HC + cols] = own[...]
    greet()
    copies = edge_copies(own, ext, HR, HC, send_sem, recv_sem)
    for copy in copies:
        copy.start()

    source = iota((cols + 2 * HC, ext_cols), 0) - HC + my_narrow * cols
    half = my_narrow * cols - HC // 2 + lax.shift_right_logical(iota((cols + 2 * HC, ext_cols), 1), 1)
    for dc in range(3):
        wanted = jnp.clip(half + (dc - 1), 0, narrow * cols - 1)
        spread_cols[:, dc * ext_cols : (dc + 1) * ext_cols] = (
            (source == wanted).astype(f32).astype(bf16)
        )
    source = iota((ext_rows, rows + 2 * HR), 1) - HR + my_wide * rows
    half = my_wide * rows - HR // 2 + lax.shift_right_logical(iota((ext_rows, rows + 2 * HR), 0), 1)
    spread_rows = jnp.concatenate(
        [
            (source == jnp.clip(half + (dr - 1), 0, wide * rows - 1)).astype(f32).astype(bf16)
            for dr in range(3)
        ],
        axis=0,
    )
    for copy in copies:
        copy.wait()

    stretched = [
        jnp.dot(ext[f].astype(bf16), spread_cols[...], preferred_element_type=f32).astype(bf16)
        for f in range(nflux)
    ]
    for f in range(nflux):
        doubled = jnp.dot(spread_rows, stretched[f], preferred_element_type=f32)
        total = None
        for code in range(9):
            dr, dc = code // 3, code % 3
            part = doubled[
                dr * ext_rows : (dr + 1) * ext_rows, dc * ext_cols : (dc + 1) * ext_cols
            ]
            term = wsum_ref[code] * part
            total = term if total is None else total + term
        forcing[f] = total

    mask = planes_ref[0]
    mask_east = mask * turned(mask, -1, 1)
    mask_north = mask * turned(mask, -1, 0)
    height, flow_u, flow_v = planes_ref[1], planes_ref[2], planes_ref[3]
    fresh = fresh_gain * forcing[1]
    stress_u = wind_gain * forcing[2]
    stress_v = wind_gain * forcing[3]
    for _ in range(NSUB):
        flow_u = mask_east * (flow_u - gravity * (turned(height, -1, 1) - height) + stress_u)
        flow_v = mask_north * (flow_v - gravity * (turned(height, -1, 0) - height) + stress_v)
        spread = (flow_u - turned(flow_u, 1, 1)) + (flow_v - turned(flow_v, 1, 0))
        height = mask * (height - depth_mean * spread + fresh)
    middle = (
        slice(HR, HR + height_ref.shape[0]),
        slice(HC, HC + height_ref.shape[1]),
    )
    heat_ref[...] = (heat_gain * mask * forcing[0])[middle]
    height_ref[...] = height[middle]
    flow_ref[0] = flow_u[middle]
    flow_ref[1] = flow_v[middle]


def params(limit=VMEM_BYTES, **more):
    return pltpu.CompilerParams(vmem_limit_bytes=limit, **more)


def per_device(
    atm_state,
    group_owner,
    regime_ops,
    flux_map,
    remap_src,
    remap_weight,
    ocean_mask,
    tracer,
    surface_height,
    transports,
):
    peers = lax.axis_size(("wide", "narrow"))
    features, columns_here = atm_state.shape
    nflux = flux_map.shape[1]
    capacity = 2 * columns_here // peers
    total_slots = peers * capacity
    sweeps = regime_ops.shape[1]
    tail = features - LANES
    entries, rows, cols = remap_src.shape
    levels = tracer.shape[0]
    shape = jax.ShapeDtypeStruct

    turned_ops = jnp.swapaxes(regime_ops[0], 1, 2)
    heads = turned_ops[:, :, :LANES].reshape(sweeps * features, LANES)
    rests = jnp.swapaxes(turned_ops[:, :, LANES:], 0, 1).reshape(features, sweeps * tail)
    rests = jnp.pad(rests, ((0, 0), (0, LANES - sweeps * tail)))
    packed = jnp.concatenate([heads, rests], axis=0)
    packed_rows = packed.shape[0]
    ext_rows, ext_cols = rows + 2 * HR, cols + 2 * HC
    padded_levels = -(-levels // 8) * 8
    gather_events = 8 * (lax.axis_size("wide") // 2)
    hbm = pl.BlockSpec(memory_space=pl.ANY)
    gathered, placed, slots, wsum, planes, tracer_mixed = pl.pallas_call(
        functools.partial(prepare_kernel, capacity),
        out_shape=(
            shape((peers,) + packed.shape, bf16),
            shape((features, total_slots), bf16),
            shape((1, columns_here), i32),
            shape((9, ext_rows, ext_cols), f32),
            shape((4, ext_rows, ext_cols), f32),
            shape(tracer.shape, f32),
        ),
        in_specs=[hbm, VMEM] + [hbm] * 7,
        out_specs=(hbm,) + (VMEM,) * 5,
        scratch_shapes=[
            pltpu.VMEM(atm_state.shape, f32),
            pltpu.VMEM(remap_src.shape, i32),
            pltpu.VMEM(remap_weight.shape, f32),
            pltpu.VMEM(ocean_mask.shape, i32),
            pltpu.VMEM(tracer.shape, f32),
            pltpu.VMEM(surface_height.shape, f32),
            pltpu.VMEM(transports.shape, f32),
            pltpu.VMEM((4 + 2 * entries, rows, cols), f32),
            pltpu.VMEM((4 + 2 * entries, ext_rows, ext_cols), f32),
            pltpu.VMEM((2, padded_levels, cols), f32),
            pltpu.VMEM((2, padded_levels, cols), f32),
            pltpu.VMEM((2, rows, LANES), f32),
            pltpu.VMEM((2, rows, LANES), f32),
            pltpu.VMEM((4, rows, cols), f32),
            pltpu.SemaphoreType.DMA((gather_events,)),
            pltpu.SemaphoreType.DMA((gather_events,)),
            pltpu.SemaphoreType.DMA((8,)),
            pltpu.SemaphoreType.DMA((8,)),
            pltpu.SemaphoreType.DMA((8,)),
            pltpu.SemaphoreType.DMA((4,)),
            pltpu.SemaphoreType.DMA((4,)),
        ],
        compiler_params=params(limit=ALL_VMEM_BYTES, collective_id=0, has_side_effects=True),
        cost_estimate=pl.CostEstimate(
            flops=2 * features * columns_here * total_slots,
            bytes_accessed=8 * tracer.size,
            transcendentals=0,
        ),
        name="prepare",
    )(
        packed,
        group_owner.reshape(1, columns_here),
        atm_state,
        remap_src,
        remap_weight,
        ocean_mask,
        tracer,
        surface_height,
        transports,
    )
    gathered = gathered.reshape(peers * packed_rows, LANES)

    groups = PHYS // capacity
    padded_map = jnp.pad(flux_map.T, ((0, 16 - nflux), (0, 0)))
    y_rows = features + 16
    answers = pl.pallas_call(
        functools.partial(physics_kernel, sweeps, capacity, packed_rows),
        grid=(total_slots // PHYS,),
        out_shape=shape((y_rows, total_slots), bf16),
        in_specs=[
            pl.BlockSpec((groups * packed_rows, LANES), lambda i: (i, 0)),
            pl.BlockSpec((features, PHYS), lambda i: (0, i)),
            pl.BlockSpec((16, features), lambda i: (0, 0)),
        ],
        out_specs=pl.BlockSpec((y_rows, PHYS), lambda i: (0, i)),
        compiler_params=params(),
        name="physics",
    )(gathered, placed, padded_map)

    atm_new, fluxes = pl.pallas_call(
        fetch_kernel,
        grid=(columns_here // CHUNK,),
        out_shape=(shape((features, columns_here), f32), shape((16, columns_here), f32)),
        in_specs=[
            pl.BlockSpec((y_rows, total_slots), lambda i: (0, 0)),
            pl.BlockSpec((1, CHUNK), lambda i: (0, i)),
            pl.BlockSpec((features, CHUNK), lambda i: (0, i)),
        ],
        out_specs=(
            pl.BlockSpec((features, CHUNK), lambda i: (0, i)),
            pl.BlockSpec((16, CHUNK), lambda i: (0, i)),
        ),
        compiler_params=params(),
        name="fetch",
    )(answers, slots, atm_state)

    block_rows = columns_here // AC
    flux_block = fluxes[:nflux].reshape(nflux, block_rows, AC)
    heat, height, flows = pl.pallas_call(
        barotropic_kernel,
        out_shape=(
            shape((rows, cols), f32),
            shape((rows, cols), f32),
            shape((2, rows, cols), f32),
        ),
        in_specs=[VMEM] * 3,
        out_specs=(VMEM,) * 3,
        scratch_shapes=[
            pltpu.VMEM((nflux, block_rows, AC), f32),
            pltpu.VMEM((nflux, block_rows + 2 * HR, AC + 2 * HC), f32),
            pltpu.VMEM((AC + 2 * HC, 3 * ext_cols), bf16),
            pltpu.VMEM((nflux, ext_rows, ext_cols), f32),
            pltpu.SemaphoreType.DMA((8,)),
            pltpu.SemaphoreType.DMA((8,)),
        ],
        compiler_params=params(collective_id=1, has_side_effects=True),
        name="barotropic",
    )(flux_block, wsum, planes)
    tracer_new = tracer_mixed.at[0].add(heat)
    return (atm_new, tracer_new, height, flows)


def solution(mesh):
    in_specs = (
        P(None, ("wide", "narrow")),
        P(("wide", "narrow"), None),
        P(("wide", "narrow"), None, None, None),
        P(),
        P(None, "wide", "narrow"),
        P(None, "wide", "narrow"),
        P("wide", "narrow"),
        P(None, "wide", "narrow"),
        P("wide", "narrow"),
        P(None, "wide", "narrow"),
    )
    out_specs = (
        P(None, ("wide", "narrow")),
        P(None, "wide", "narrow"),
        P("wide", "narrow"),
        P(None, "wide", "narrow"),
    )
    return jax.shard_map(
        per_device, mesh=mesh, in_specs=in_specs, out_specs=out_specs, check_vma=False
    )
```

```python
import functools

import jax
import jax.numpy as jnp
from jax import lax
from jax.experimental import pallas as pl
from jax.experimental.pallas import tpu as pltpu
from jax.sharding import PartitionSpec as P

AC = 128
PHYS = 1024
NSUB = 4
LANES = 128
CHUNK = 512
VMEM_BYTES = 48 * 1024 * 1024
ALL_VMEM_BYTES = 60 * 1024 * 1024

relax_rate = 0.5
kappa_mix = 0.2
heat_gain = 0.5
gravity = 0.7
depth_mean = 0.7
wind_gain = 0.3
fresh_gain = 0.3

f32 = jnp.float32
bf16 = jnp.bfloat16
i32 = jnp.int32
MESH = pl.DeviceIdType.MESH
SIDES = ((1, 0), (-1, 0), (0, 1), (0, -1), (1, 1), (1, -1), (-1, 1), (-1, -1))
VMEM = pl.BlockSpec(memory_space=pltpu.VMEM)


def iota(shape, dim):
    return lax.broadcasted_iota(i32, shape, dim)


def physics_kernel(sweeps, capacity, packed_rows, ops_ref, xs_ref, fm_ref, y_ref):
    features = xs_ref.shape[0]
    tail = features - LANES
    groups = PHYS // capacity
    initial = [xs_ref[:, g * capacity : (g + 1) * capacity].astype(f32) for g in range(groups)]
    current = list(initial)
    for sweep in range(sweeps):
        for g in range(groups):
            base = g * packed_rows
            rounded = current[g].astype(bf16)
            parts = [rounded[:LANES]]
            if sweep > 0:
                parts.append(jnp.zeros((sweep * tail, capacity), bf16))
            parts.append(rounded[LANES:])
            parts.append(jnp.zeros((LANES - (sweep + 1) * tail, capacity), bf16))
            operand = jnp.concatenate(parts, axis=0)
            head = ops_ref[base + sweep * features : base + (sweep + 1) * features, :]
            rest = ops_ref[base + sweeps * features : base + (sweeps + 1) * features, :]
            matrix = jnp.concatenate([head, rest], axis=1)
            mixed = jnp.dot(matrix, operand, preferred_element_type=f32)
            current[g] = current[g] + relax_rate * jnp.tanh(mixed)
    for g in range(groups):
        cols = slice(g * capacity, (g + 1) * capacity)
        y_ref[:features, cols] = (current[g] - initial[g]).astype(bf16)
        fluxes = jnp.dot(fm_ref[...], current[g].astype(bf16), preferred_element_type=f32)
        y_ref[features:, cols] = fluxes.astype(bf16)


def fetch_kernel(y_ref, slot_ref, atm_ref, new_ref, flux_ref):
    features = atm_ref.shape[0]
    slots = y_ref.shape[1]
    selector = (iota((slots, slot_ref.shape[1]), 0) == slot_ref[...]).astype(f32).astype(bf16)
    returned = jnp.dot(y_ref[...], selector, preferred_element_type=f32)
    new_ref[...] = atm_ref[...] + returned[:features]
    flux_ref[...] = returned[features:]


def side_device(side):
    wide, narrow = lax.axis_size("wide"), lax.axis_size("narrow")
    return (
        lax.rem(lax.axis_index("wide") + side[0] + wide, wide),
        lax.rem(lax.axis_index("narrow") + side[1] + narrow, narrow),
    )


def greet(sides=SIDES):
    barrier = pltpu.get_barrier_semaphore()
    for side in sides:
        pl.semaphore_signal(barrier, inc=1, device_id=side_device(side), device_id_type=MESH)
    pl.semaphore_wait(barrier, len(sides))


def leaving(step, size, halo):
    if step > 0:
        return pl.ds(size - halo, halo)
    return pl.ds(0, halo) if step < 0 else pl.ds(0, size)


def landing(step, size, halo):
    if step > 0:
        return pl.ds(0, halo)
    return pl.ds(halo + size, halo) if step < 0 else pl.ds(halo, size)


def edge_copies(src, dst, halo_rows, halo_cols, send_sem, recv_sem):
    rows, cols = src.shape[1], src.shape[2]
    return [
        pltpu.make_async_remote_copy(
            src_ref=src.at[:, leaving(dr, rows, halo_rows), leaving(dc, cols, halo_cols)],
            dst_ref=dst.at[:, landing(dr, rows, halo_rows), landing(dc, cols, halo_cols)],
            send_sem=send_sem.at[k],
            recv_sem=recv_sem.at[k],
            device_id=side_device((dr, dc)),
            device_id_type=MESH,
        )
        for k, (dr, dc) in enumerate(SIDES)
    ]


HR = 8
HC = 128


def turned(x, shift, axis):
    return pltpu.roll(x, shift % x.shape[axis], axis)


class Gather:
    def __init__(self, packed, slots, send_sem, recv_sem):
        self.packed, self.slots = packed, slots
        self.send_sem, self.recv_sem = send_sem, recv_sem
        wide, self.narrow = lax.axis_size("wide"), lax.axis_size("narrow")
        self.zs = wide // 2
        w, n = lax.axis_index("wide"), lax.axis_index("narrow")
        self.z, self.y, self.x, self.c = w // 2, lax.rem(w, 2), n // 2, lax.rem(n, 2)
        self.offsets = [0]
        for d in range(1, self.zs // 2 + 1):
            self.offsets += [-d, d] if d < self.zs - d else [-d]
        self.sent = {}

    def index(self, kind, k):
        z = lax.rem(self.z + self.offsets[k] + self.zs, self.zs)
        y = 1 - self.y if kind in "yd" else self.y
        x = 1 - self.x if kind in "xd" else self.x
        return (z * 2 + y) * self.narrow + x * 2 + self.c

    def place(self, way):
        z = lax.rem(self.z + way.get("z", 0) + self.zs, self.zs)
        y = 1 - self.y if "y" in way else self.y
        x = 1 - self.x if "x" in way else self.x
        c = 1 - self.c if "c" in way else self.c
        return z * 2 + y, x * 2 + c

    def number(self, kind, k):
        if kind[0] == "c":
            return 4 * self.zs + self.number(kind[1], k)
        return "zxyd".index(kind) * self.zs + k

    def send(self, have, k, kind, to, way):
        at = self.index(have, k)
        event = self.number(kind, to)
        copy = pltpu.make_async_remote_copy(
            src_ref=self.packed if have == "z" and k == 0 else self.slots.at[at],
            dst_ref=self.slots.at[at],
            send_sem=self.send_sem.at[event],
            recv_sem=self.recv_sem.at[event],
            device_id=self.place(way),
            device_id_type=MESH,
        )
        copy.start()
        self.sent[kind, to] = copy

    def onward(self, kind, k):
        if kind == "z":
            d = self.offsets[k]
            if d <= 0 and d - 1 in self.offsets:
                self.send("z", k, "z", self.offsets.index(d - 1), {"z": 1})
            if d >= 0 and d + 1 in self.offsets:
                self.send("z", k, "z", self.offsets.index(d + 1), {"z": -1})
            self.send("z", k, "x", k, {"x": 1})
            self.send("z", k, "y", k, {"y": 1})
        elif kind == "x" and k % 2 == 0:
            self.send("x", k, "d", k, {"y": 1})
        elif kind == "y" and k % 2 == 1:
            self.send("y", k, "d", k, {"x": 1})
        self.send(kind, k, "c" + kind, k, {"c": 1})

    def arrive(self, kind, k):
        self.sent[kind, k].wait_recv()
        if kind[0] != "c":
            self.onward(kind, k)

    def rounds(self):
        steps = []
        for k in range(self.zs):
            if k > 0:
                steps.append([("z", k)])
                steps.append([("x", k - 1), ("y", k - 1)])
        steps.append([("x", self.zs - 1), ("y", self.zs - 1)])
        for k in range(self.zs):
            steps.append([("d", k)])
        return steps


AROUND = SIDES + ((2, 0), (-2, 0), (0, 2))


def prepare_kernel(
    capacity,
    packed_hbm, owner_ref, atm_hbm, src_hbm, weight_hbm, mask_hbm, tracer_hbm, height_hbm, flow_hbm,
    slots_hbm, xs_ref, slot_ref, wsum_ref, planes_ref, tracer_out_ref,
    atm_ref, src_ref, weight_ref, mask_ref, tracer_ref, height_ref, flow_ref,
    own, ext, row_out, row_in, col_out, col_in, coef,
    gsend_sem, grecv_sem, load_sem, send_sem, recv_sem, tsend_sem, trecv_sem,
):
    entries, rows, cols = src_ref.shape
    levels = tracer_ref.shape[0]
    wide, narrow = lax.axis_size("wide"), lax.axis_size("narrow")
    peers = wide * narrow
    gather = Gather(packed_hbm, slots_hbm, gsend_sem, grecv_sem)
    loads = [
        pltpu.make_async_copy(a, b, load_sem.at[k])
        for k, (a, b) in enumerate(
            (
                (mask_hbm, mask_ref),
                (height_hbm, height_ref),
                (flow_hbm, flow_ref),
                (src_hbm, src_ref),
                (weight_hbm, weight_ref),
                (tracer_hbm, tracer_ref),
                (atm_hbm, atm_ref),
                (packed_hbm, slots_hbm.at[gather.index("z", 0)]),
            )
        )
    ]
    for load in loads:
        load.start()
    greet(AROUND)
    gather.onward("z", 0)

    for load in loads[:5]:
        load.wait()
    own[0] = mask_ref[...].astype(f32)
    own[1] = height_ref[...]
    own[2] = flow_ref[0]
    own[3] = flow_ref[1]
    for e in range(entries):
        own[4 + e] = src_ref[e].astype(f32)
        own[4 + entries + e] = weight_ref[e]
    ext[:, HR : HR + rows, HC : HC + cols] = own[...]
    copies = edge_copies(own, ext, HR, HC, send_sem, recv_sem)
    for copy in copies:
        copy.start()
    loads[5].wait()

    lane = iota((rows, LANES), 1)

    def pack(level, carry):
        first, last = carry
        field = tracer_ref[level]
        row_out[0, pl.ds(level, 1), :] = field[rows - 1 : rows, :]
        row_out[1, pl.ds(level, 1), :] = field[0:1, :]
        first = jnp.where(lane == level, field[:, 0:1], first)
        last = jnp.where(lane == level, field[:, cols - 1 : cols], last)
        return first, last

    blank = jnp.zeros((rows, LANES), f32)
    first, last = lax.fori_loop(0, levels, pack, (blank, blank))
    for spare in range(levels, row_out.shape[1]):
        for k in range(2):
            row_out[k, spare : spare + 1, :] = jnp.zeros((1, cols), f32)
    col_out[0] = last
    col_out[1] = first
    tcopies = []
    for k in range(4):
        out, into = (row_out, row_in) if k < 2 else (col_out, col_in)
        tcopies.append(
            pltpu.make_async_remote_copy(
                src_ref=out.at[k % 2],
                dst_ref=into.at[k % 2],
                send_sem=tsend_sem.at[k],
                recv_sem=trecv_sem.at[k],
                device_id=side_device(SIDES[k]),
                device_id_type=MESH,
            )
        )
    for copy in tcopies:
        copy.start()

    def rank():
        loads[6].wait()
        loads[7].wait()
        count = owner_ref.shape[1]
        upper = (iota((LANES, LANES), 0) < iota((LANES, LANES), 1)).astype(f32).astype(bf16)
        ids = iota((peers, LANES), 0)
        carry = jnp.zeros((peers, 1), f32)
        for start in range(0, count, LANES):
            owner = owner_ref[:, start : start + LANES]
            hot = (ids == owner).astype(f32)
            before = jnp.dot(hot.astype(bf16), upper, preferred_element_type=f32) + carry
            ranks = jnp.sum(hot * before, axis=0, keepdims=True)
            slot_ref[:, start : start + LANES] = owner * capacity + ranks.astype(i32)
            carry = carry + jnp.sum(hot, axis=1, keepdims=True)

    def place(first, last):
        columns = atm_ref[...].astype(bf16)

        def step(i, _):
            begin = pl.multiple_of(i * CHUNK, CHUNK)
            selector = (iota((CHUNK, slot_ref.shape[1]), 0) + begin == slot_ref[...]).astype(f32)
            placed = lax.dot_general(
                columns, selector.astype(bf16), (((1,), (1,)), ((), ())), preferred_element_type=f32
            )
            xs_ref[:, pl.ds(begin, CHUNK)] = placed.astype(bf16)
            return 0

        lax.fori_loop(first, last, step, 0)

    middle = (slice(HR, HR + rows), slice(HC, HC + cols))
    ext_rows, ext_cols = ext.shape[1], ext.shape[2]

    def planes():
        for copy in copies:
            copy.wait()
        row = iota((ext_rows, ext_cols), 0) + (lax.axis_index("wide") * rows - HR)
        col = iota((ext_rows, ext_cols), 1) + (lax.axis_index("narrow") * cols - HC)
        inside = (row >= 0) & (row < wide * rows) & (col >= 0) & (col < narrow * cols)
        mask = jnp.where(inside, ext[0], 0.0)
        planes_ref[0] = mask
        planes_ref[1] = ext[1]
        planes_ref[2] = ext[2]
        planes_ref[3] = ext[3]
        for k, (shift, axis) in enumerate(((-1, 0), (1, 0), (-1, 1), (1, 1))):
            coef[k] = (kappa_mix * mask * turned(mask, shift, axis))[middle]

    def weights(first, last):
        for slab in range(first, last, 8):
            at = slice(slab, slab + 8)
            codes = [ext[4 + e, at, :] for e in range(entries)]
            parts = [ext[4 + entries + e, at, :] for e in range(entries)]
            for code in range(9):
                total = jnp.where(codes[0] == code, parts[0], 0.0)
                for e in range(1, entries):
                    total = total + jnp.where(codes[e] == code, parts[e], 0.0)
                wsum_ref[code, at, :] = total

    row = iota((rows, cols), 0)
    col = iota((rows, cols), 1)

    def diffuse(level, _):
        field = tracer_ref[level]
        here = lane == level
        south = jnp.where(row == 0, row_in[0, pl.ds(level, 1), :], turned(field, 1, 0))
        north = jnp.where(row == rows - 1, row_in[1, pl.ds(level, 1), :], turned(field, -1, 0))
        west_edge = jnp.sum(jnp.where(here, col_in[0], 0.0), axis=1, keepdims=True)
        east_edge = jnp.sum(jnp.where(here, col_in[1], 0.0), axis=1, keepdims=True)
        west = jnp.where(col == 0, west_edge, turned(field, 1, 1))
        east = jnp.where(col == cols - 1, east_edge, turned(field, -1, 1))
        tracer_out_ref[level] = field + (
            coef[0] * (north - field)
            + coef[1] * (south - field)
            + coef[2] * (east - field)
            + coef[3] * (west - field)
        )
        return 0

    def mix(first, last):
        if first == 0:
            for copy in tcopies:
                copy.wait()
        lax.fori_loop(first, last, diffuse, 0)

    chunks = xs_ref.shape[1] // CHUNK
    work = [rank]
    work += [functools.partial(place, i, min(i + 2, chunks)) for i in range(0, chunks, 2)]
    work += [planes]
    work += [functools.partial(weights, i, i + 16) for i in range(0, ext_rows, 16)]
    work += [functools.partial(mix, i, min(i + 16, levels)) for i in range(0, levels, 16)]
    for events in gather.rounds():
        if work:
            work.pop(0)()
        for event in events:
            gather.arrive(*event)
    while work:
        work.pop(0)()
    for kind in "zxyd":
        for k in range(gather.zs):
            gather.arrive("c" + kind, k)
    for copy in gather.sent.values():
        copy.wait_send()


def barotropic_kernel(
    flux_ref, wsum_ref, planes_ref,
    heat_ref, height_ref, flow_ref,
    own, ext, spread_cols, forcing, send_sem, recv_sem,
):
    nflux, rows, cols = flux_ref.shape
    ext_rows, ext_cols = planes_ref.shape[1], planes_ref.shape[2]
    wide, narrow = lax.axis_size("wide"), lax.axis_size("narrow")
    my_wide, my_narrow = lax.axis_index("wide"), lax.axis_index("narrow")
    own[...] = flux_ref[...]
    ext[:, HR : HR + rows, HC : HC + cols] = own[...]
    greet()
    copies = edge_copies(own, ext, HR, HC, send_sem, recv_sem)
    for copy in copies:
        copy.start()

    source = iota((cols + 2 * HC, ext_cols), 0) - HC + my_narrow * cols
    half = my_narrow * cols - HC // 2 + lax.shift_right_logical(iota((cols + 2 * HC, ext_cols), 1), 1)
    for dc in range(3):
        wanted = jnp.clip(half + (dc - 1), 0, narrow * cols - 1)
        spread_cols[:, dc * ext_cols : (dc + 1) * ext_cols] = (
            (source == wanted).astype(f32).astype(bf16)
        )
    source = iota((ext_rows, rows + 2 * HR), 1) - HR + my_wide * rows
    half = my_wide * rows - HR // 2 + lax.shift_right_logical(iota((ext_rows, rows + 2 * HR), 0), 1)
    spread_rows = jnp.concatenate(
        [
            (source == jnp.clip(half + (dr - 1), 0, wide * rows - 1)).astype(f32).astype(bf16)
            for dr in range(3)
        ],
        axis=0,
    )
    for copy in copies:
        copy.wait()

    stretched = [
        jnp.dot(ext[f].astype(bf16), spread_cols[...], preferred_element_type=f32).astype(bf16)
        for f in range(nflux)
    ]
    for f in range(nflux):
        doubled = jnp.dot(spread_rows, stretched[f], preferred_element_type=f32)
        total = None
        for code in range(9):
            dr, dc = code // 3, code % 3
            part = doubled[
                dr * ext_rows : (dr + 1) * ext_rows, dc * ext_cols : (dc + 1) * ext_cols
            ]
            term = wsum_ref[code] * part
            total = term if total is None else total + term
        forcing[f] = total

    mask = planes_ref[0]
    mask_east = mask * turned(mask, -1, 1)
    mask_north = mask * turned(mask, -1, 0)
    height, flow_u, flow_v = planes_ref[1], planes_ref[2], planes_ref[3]
    fresh = fresh_gain * forcing[1]
    stress_u = wind_gain * forcing[2]
    stress_v = wind_gain * forcing[3]
    for _ in range(NSUB):
        flow_u = mask_east * (flow_u - gravity * (turned(height, -1, 1) - height) + stress_u)
        flow_v = mask_north * (flow_v - gravity * (turned(height, -1, 0) - height) + stress_v)
        spread = (flow_u - turned(flow_u, 1, 1)) + (flow_v - turned(flow_v, 1, 0))
        height = mask * (height - depth_mean * spread + fresh)
    middle = (
        slice(HR, HR + height_ref.shape[0]),
        slice(HC, HC + height_ref.shape[1]),
    )
    heat_ref[...] = (heat_gain * mask * forcing[0])[middle]
    height_ref[...] = height[middle]
    flow_ref[0] = flow_u[middle]
    flow_ref[1] = flow_v[middle]


def params(limit=VMEM_BYTES, **more):
    return pltpu.CompilerParams(vmem_limit_bytes=limit, **more)


def per_device(
    atm_state,
    group_owner,
    regime_ops,
    flux_map,
    remap_src,
    remap_weight,
    ocean_mask,
    tracer,
    surface_height,
    transports,
):
    peers = lax.axis_size(("wide", "narrow"))
    features, columns_here = atm_state.shape
    nflux = flux_map.shape[1]
    capacity = 2 * columns_here // peers
    total_slots = peers * capacity
    sweeps = regime_ops.shape[1]
    tail = features - LANES
    entries, rows, cols = remap_src.shape
    levels = tracer.shape[0]
    shape = jax.ShapeDtypeStruct

    turned_ops = jnp.swapaxes(regime_ops[0], 1, 2)
    heads = turned_ops[:, :, :LANES].reshape(sweeps * features, LANES)
    rests = jnp.swapaxes(turned_ops[:, :, LANES:], 0, 1).reshape(features, sweeps * tail)
    rests = jnp.pad(rests, ((0, 0), (0, LANES - sweeps * tail)))
    packed = jnp.concatenate([heads, rests], axis=0)
    packed_rows = packed.shape[0]
    ext_rows, ext_cols = rows + 2 * HR, cols + 2 * HC
    padded_levels = -(-levels // 8) * 8
    gather_events = 8 * (lax.axis_size("wide") // 2)
    hbm = pl.BlockSpec(memory_space=pl.ANY)
    gathered, placed, slots, wsum, planes, tracer_mixed = pl.pallas_call(
        functools.partial(prepare_kernel, capacity),
        out_shape=(
            shape((peers,) + packed.shape, bf16),
            shape((features, total_slots), bf16),
            shape((1, columns_here), i32),
            shape((9, ext_rows, ext_cols), f32),
            shape((4, ext_rows, ext_cols), f32),
            shape(tracer.shape, f32),
        ),
        in_specs=[hbm, VMEM] + [hbm] * 7,
        out_specs=(hbm,) + (VMEM,) * 5,
        scratch_shapes=[
            pltpu.VMEM(atm_state.shape, f32),
            pltpu.VMEM(remap_src.shape, i32),
            pltpu.VMEM(remap_weight.shape, f32),
            pltpu.VMEM(ocean_mask.shape, i32),
            pltpu.VMEM(tracer.shape, f32),
            pltpu.VMEM(surface_height.shape, f32),
            pltpu.VMEM(transports.shape, f32),
            pltpu.VMEM((4 + 2 * entries, rows, cols), f32),
            pltpu.VMEM((4 + 2 * entries, ext_rows, ext_cols), f32),
            pltpu.VMEM((2, padded_levels, cols), f32),
            pltpu.VMEM((2, padded_levels, cols), f32),
            pltpu.VMEM((2, rows, LANES), f32),
            pltpu.VMEM((2, rows, LANES), f32),
            pltpu.VMEM((4, rows, cols), f32),
            pltpu.SemaphoreType.DMA((gather_events,)),
            pltpu.SemaphoreType.DMA((gather_events,)),
            pltpu.SemaphoreType.DMA((8,)),
            pltpu.SemaphoreType.DMA((8,)),
            pltpu.SemaphoreType.DMA((8,)),
            pltpu.SemaphoreType.DMA((4,)),
            pltpu.SemaphoreType.DMA((4,)),
        ],
        compiler_params=params(limit=ALL_VMEM_BYTES, collective_id=0, has_side_effects=True),
        cost_estimate=pl.CostEstimate(
            flops=2 * features * columns_here * total_slots,
            bytes_accessed=8 * tracer.size,
            transcendentals=0,
        ),
        name="prepare",
    )(
        packed,
        group_owner.reshape(1, columns_here),
        atm_state,
        remap_src,
        remap_weight,
        ocean_mask,
        tracer,
        surface_height,
        transports,
    )
    gathered = gathered.reshape(peers * packed_rows, LANES)

    groups = PHYS // capacity
    padded_map = jnp.pad(flux_map.T, ((0, 16 - nflux), (0, 0)))
    y_rows = features + 16
    answers = pl.pallas_call(
        functools.partial(physics_kernel, sweeps, capacity, packed_rows),
        grid=(total_slots // PHYS,),
        out_shape=shape((y_rows, total_slots), bf16),
        in_specs=[
            pl.BlockSpec((groups * packed_rows, LANES), lambda i: (i, 0)),
            pl.BlockSpec((features, PHYS), lambda i: (0, i)),
            pl.BlockSpec((16, features), lambda i: (0, 0)),
        ],
        out_specs=pl.BlockSpec((y_rows, PHYS), lambda i: (0, i)),
        compiler_params=params(),
        name="physics",
    )(gathered, placed, padded_map)

    atm_new, fluxes = pl.pallas_call(
        fetch_kernel,
        grid=(columns_here // CHUNK,),
        out_shape=(shape((features, columns_here), f32), shape((16, columns_here), f32)),
        in_specs=[
            pl.BlockSpec((y_rows, total_slots), lambda i: (0, 0)),
            pl.BlockSpec((1, CHUNK), lambda i: (0, i)),
            pl.BlockSpec((features, CHUNK), lambda i: (0, i)),
        ],
        out_specs=(
            pl.BlockSpec((features, CHUNK), lambda i: (0, i)),
            pl.BlockSpec((16, CHUNK), lambda i: (0, i)),
        ),
        compiler_params=params(),
        name="fetch",
    )(answers, slots, atm_state)

    block_rows = columns_here // AC
    flux_block = fluxes[:nflux].reshape(nflux, block_rows, AC)
    heat, height, flows = pl.pallas_call(
        barotropic_kernel,
        out_shape=(
            shape((rows, cols), f32),
            shape((rows, cols), f32),
            shape((2, rows, cols), f32),
        ),
        in_specs=[VMEM] * 3,
        out_specs=(VMEM,) * 3,
        scratch_shapes=[
            pltpu.VMEM((nflux, block_rows, AC), f32),
            pltpu.VMEM((nflux, block_rows + 2 * HR, AC + 2 * HC), f32),
            pltpu.VMEM((AC + 2 * HC, 3 * ext_cols), bf16),
            pltpu.VMEM((nflux, ext_rows, ext_cols), f32),
            pltpu.SemaphoreType.DMA((8,)),
            pltpu.SemaphoreType.DMA((8,)),
        ],
        compiler_params=params(collective_id=1, has_side_effects=True),
        name="barotropic",
    )(flux_block, wsum, planes)
    tracer_new = tracer_mixed.at[0].add(heat)
    return (atm_new, tracer_new, height, flows)


def solution(mesh):
    in_specs = (
        P(None, ("wide", "narrow")),
        P(("wide", "narrow"), None),
        P(("wide", "narrow"), None, None, None),
        P(),
        P(None, "wide", "narrow"),
        P(None, "wide", "narrow"),
        P("wide", "narrow"),
        P(None, "wide", "narrow"),
        P("wide", "narrow"),
        P(None, "wide", "narrow"),
    )
    out_specs = (
        P(None, ("wide", "narrow")),
        P(None, "wide", "narrow"),
        P("wide", "narrow"),
        P(None, "wide", "narrow"),
    )
    return jax.shard_map(
        per_device, mesh=mesh, in_specs=in_specs, out_specs=out_specs, check_vma=False
    )
```
